128 devices in a mesh: head: 4 (over x), ctx: 32 (over y, z, core).
Axes of the slice: x: 4, y: 4, z: 4, core: 2. Of those that a mesh axis runs over, the one named last changes fastest.
Arguments:
- qkv: bfloat16 [12288, 3, 1024], P(('ctx', 'head')), may hold values from -6 to 6
- grad_out: bfloat16 [12288, 1024], P(('ctx', 'head')), may hold values from -6 to 6
- rab: float32 [16, 20], replicated, may hold values from -3 to 3
- doc_ids: int32 [12288], replicated, may hold values from 0 to 7, never falling along the last dimension, each value on 1 to 6144 neighbouring positions
Outputs:
- attn_out: bfloat16 [12288, 1024], P(('ctx', 'head'))
- grad_qkv: bfloat16 [12288, 3, 1024], P(('ctx', 'head'))
- grad_rab: float32 [16, 20], P('head')
The draws below stay inside these ranges and needn't reach their ends.
Inputs may be any that keep to these rules, and one draw needn't show every extreme that they name: `doc_ids`: 12288 events of 8 user histories laid end to end: history numbers never fall, every history has 1 to 6144 events, one has exactly 6144.
All inputs are finite; a program needn't handle non-finite values.
Results may differ from the reference program's by a relative error of at most 0.014.
Values may be sent and summed in bfloat16 or wider, within the bound.
No kernel may reach another device: no remote copies, remote signals or barrier semaphores. Data moves between devices by JAX's collectives and lax.ppermute only.
A program may use at most 128 MiB of HBM per device.

```python
import math
import jax
import jax.numpy as jnp
import numpy as np
from jax import lax

D = 1024
H = 16
HD = 64
NB = 20
DOCS = 8
TOTAL = 12288
MAXLEN = 6144


def shard_levels(key, shape, split, smallest, largest):
    loudness, own = 1.0, jax.random.fold_in(key, 6)
    for position, parts in split:
        heights = jnp.exp(jax.random.uniform(jax.random.fold_in(own, position), (parts,), jnp.float32, smallest / len(split), largest / len(split)))
        loudness = loudness * jnp.repeat(heights, shape[position] // parts).reshape([-1 if axis == position else 1 for axis in range(len(shape))])
    return loudness


def profile(amount, total, most, skew):
    portions = [(1 << 20) // math.isqrt(standing ** skew) + 1 for standing in range(2, amount + 1)]
    spare, holding = total - most - (amount - 1), [1] * (amount - 1)
    while spare > 0:
        free = [i for i in range(amount - 1) if holding[i] < most]
        whole, remaining = sum([portions[i] for i in free]), spare
        for i in free:
            extra = min(most - holding[i], max(1, remaining * portions[i] // whole), spare)
            holding[i] = holding[i] + extra
            spare = spare - extra
    return np.array([most] + holding)


def uneven_parts(stream_key, count, total, most, lean):
    if count == 2:
        one = jax.random.randint(stream_key, (), max(1, total - most), min(most, total - 1) + 1)
        return jnp.stack([one, total - one])
    tallies = jnp.asarray(profile(count, total, most, lean), jnp.int32)
    pairs = (count - 1) // 2
    donor, receiver = tallies[1:1 + 2 * pairs:2], tallies[2:2 + 2 * pairs:2]
    slack = jnp.minimum(donor - 1, most - receiver)
    shifted = jax.random.randint(jax.random.fold_in(stream_key, 1), (pairs,), 0, 1 << 20) % (slack + 1)
    tallies = tallies.at[1:1 + 2 * pairs:2].set(donor - shifted).at[2:2 + 2 * pairs:2].set(receiver + shifted)
    return tallies[jax.random.permutation(jax.random.fold_in(stream_key, 2), count)]


def noise(own_key, shape, scale, most, shards=(), kind=jnp.bfloat16):
    gain = shard_levels(own_key, shape, shards, -0.22, 0.18) if shards else 1.0
    entries = jax.random.normal(own_key, shape, jnp.float32) * scale * gain
    return jnp.minimum(jnp.maximum(entries, -most), most).astype(kind)


def setup_inputs(seed: int = 0) -> dict:
    splits = jax.random.split(jax.random.key(seed), 5)
    qkv = noise(splits[0], (TOTAL, 3, D), 1.0, 6.0, ((0, 128),))
    grad_out = noise(splits[1], (TOTAL, D), 1.0, 6.0, ((0, 128),))
    rab = noise(splits[2], (H, NB), 1.0, 3.0, (), jnp.float32)
    doc_ids = jnp.searchsorted(jnp.cumsum(uneven_parts(splits[3], DOCS, TOTAL, MAXLEN, 2)), jnp.arange(TOTAL), side="right").astype(jnp.int32)
    return {"qkv": qkv, "grad_out": grad_out, "rab": rab, "doc_ids": doc_ids}


def bucket_of(distance):
    clipped = jnp.maximum(distance, 0)
    bucket = jnp.minimum(clipped, 8)
    for power in range(3, 14):
        bucket = bucket + (clipped >= 2 ** power).astype(jnp.int32)
    return bucket

def reference(qkv, grad_out, rab, doc_ids):
    total = doc_ids.shape[0]
    alpha = HD ** (-0.5)
    hi = lax.Precision.HIGHEST
    query_heads = qkv[:, 0].astype(jnp.float32).reshape(total, H, HD)
    key_heads = qkv[:, 1].astype(jnp.float32).reshape(total, H, HD)
    value_heads = qkv[:, 2].astype(jnp.float32).reshape(total, H, HD)
    grad_heads = grad_out.astype(jnp.float32).reshape(total, H, HD)
    counted = lax.optimization_barrier(jnp.sum((doc_ids[None, :] == jnp.arange(DOCS, dtype=jnp.int32)[:, None]).astype(jnp.float32), axis=1))
    inverse = lax.rsqrt(counted)
    scale_all = inverse[doc_ids]
    positions = jnp.arange(total, dtype=jnp.int32)
    size = math.gcd(total, 128)

    def block_step(state, index):
        key_acc, value_acc, bias_running_sum = state
        start = (index * size).astype(jnp.int32)
        qb = lax.dynamic_slice_in_dim(query_heads, start, size, 0)
        gb = lax.dynamic_slice_in_dim(grad_heads, start, size, 0)
        doc_b = lax.dynamic_slice_in_dim(doc_ids, start, size, 0)
        scale_b = lax.dynamic_slice_in_dim(scale_all, start, size, 0)
        pos_b = start + jnp.arange(size, dtype=jnp.int32)
        buckets = bucket_of(pos_b[:, None] - positions[None, :])
        attention_scores = jnp.einsum('qhd,khd->hqk', qb, key_heads, precision=hi) * alpha
        attention_scores = attention_scores + rab[:, buckets]
        allowed = (doc_b[:, None] == doc_ids[None, :]) & (positions[None, :] <= pos_b[:, None])
        signal = jax.nn.sigmoid(attention_scores)
        weights = (jnp.where(allowed, attention_scores * signal, 0.0) * scale_b[None, :, None]).astype(jnp.bfloat16).astype(jnp.float32)
        out_b = jnp.einsum('hqk,khd->qhd', weights, value_heads, precision=hi)
        direct = jnp.einsum('qhd,khd->hqk', gb, value_heads, precision=hi)
        slope = signal * (1.0 + attention_scores * (1.0 - signal))
        score_gradient = jnp.where(allowed, direct * slope, 0.0) * scale_b[None, :, None]
        dlow = score_gradient.astype(jnp.bfloat16).astype(jnp.float32)
        dq_b = jnp.einsum('hqk,khd->qhd', dlow, key_heads, precision=hi) * alpha
        key_acc = key_acc + jnp.einsum('hqk,qhd->khd', dlow, qb, precision=hi) * alpha
        value_acc = value_acc + jnp.einsum('hqk,qhd->khd', weights, gb, precision=hi)
        flat = buckets.reshape(-1)
        bias_running_sum = bias_running_sum + jax.vmap(lambda row: jax.ops.segment_sum(row.reshape(-1), flat, num_segments=NB))(score_gradient)
        return ((key_acc, value_acc, bias_running_sum), (out_b.astype(jnp.bfloat16), dq_b.astype(jnp.bfloat16)))
    start_state = (jnp.zeros((total, H, HD), jnp.float32), jnp.zeros((total, H, HD), jnp.float32), jnp.zeros((H, NB), jnp.float32))
    final, stacked = lax.scan(block_step, start_state, jnp.arange(total // size, dtype=jnp.int32))
    key_acc, value_acc, bias_running_sum = final
    attn_out = stacked[0].reshape(total, D)
    dq = stacked[1].reshape(total, D)
    dk = key_acc.reshape(total, D).astype(jnp.bfloat16)
    dv = value_acc.reshape(total, D).astype(jnp.bfloat16)
    grad_qkv = jnp.stack([dq, dk, dv], axis=1)
    return (attn_out, grad_qkv, bias_running_sum)
```

```python
import jax
import jax.numpy as jnp
from jax import lax
from jax.experimental import pallas as pl
from jax.experimental.pallas import tpu as pltpu
from jax.sharding import Mesh
from jax.sharding import PartitionSpec as P

HD = 64
H = 16
NB = 20
DOCS = 8
ROWS = 96
SUPER = 384
GROUPS = 16
CLASSES = 19
LOW = -1e30
VMEM = pltpu.VMEM
SMEM = pltpu.SMEM
NT = (((1,), (1,)), ((), ()))


def doc_bounds(ids):
    return [jnp.int32(0)] + [
        jnp.sum((ids < d).astype(jnp.float32)).astype(jnp.int32) for d in range(1, DOCS)
    ]


def pack_kernel(where_ref, ids_ref, qkv_ref, g_ref, kv_ref, qg_ref, bounds_ref):
    bounds = doc_bounds(ids_ref[...])
    for d in range(DOCS):
        bounds_ref[d] = bounds[d]
    pos = where_ref[0] + lax.broadcasted_iota(jnp.int32, (ROWS, 128), 0)
    length = jnp.zeros((ROWS, 128), jnp.int32)
    ends = bounds[1:] + [jnp.int32(SUPER * 2 * GROUPS)]
    for d in range(DOCS):
        length = jnp.where(pos >= bounds[d], ends[d] - bounds[d], length)
    scale = lax.rsqrt(length.astype(jnp.float32))[:, :HD]
    for h in range(H):
        cols = slice(h * HD, (h + 1) * HD)
        kv_ref[h] = jnp.concatenate([qkv_ref[:, 1, cols], qkv_ref[:, 2, cols]], axis=1)
        q = (qkv_ref[:, 0, cols].astype(jnp.float32) * 0.0625).astype(jnp.bfloat16)
        g = (g_ref[:, cols].astype(jnp.float32) * scale).astype(jnp.bfloat16)
        qg_ref[h] = jnp.concatenate([q, g], axis=1)


def bucket_scalar(d):
    b = jnp.minimum(d, 8)
    for p in range(3, 14):
        b = b + (d >= 2**p).astype(jnp.int32)
    return b


def next_power(d):
    b = jnp.int32(8)
    for p in range(3, 14):
        b = jnp.where(d >= 2**p, jnp.int32(2 ** (p + 1)), b)
    return b


def main_kernel(
    where_ref, bounds_ref, rab_ref,
    kv0, kv1, kv2, kv3, own_ref, other_ref,
    d0, d1, d2, d3, mine_ref, theirs_ref, bias_ref,
    kvs, qs, table, biasacc, dkv, start_ref, scale_ref, acc, lhs, qgt, buckets,
):
    x = where_ref[0]
    core = where_ref[1]
    for r, ref in enumerate((kv0, kv1, kv2, kv3)):
        at = pl.multiple_of(lax.rem(x + r, 4) * ROWS, ROWS)

        @pl.loop(0, GROUPS)
        def _(n):
            kvs[n, pl.ds(at, ROWS), :] = ref[n]

    mine_at = pl.multiple_of(core * ROWS, ROWS)
    theirs_at = pl.multiple_of((1 - core) * ROWS, ROWS)

    @pl.loop(0, GROUPS)
    def _(n):
        qs[n, pl.ds(mine_at, ROWS), :] = own_ref[n]
        qs[n, pl.ds(theirs_at, ROWS), :] = other_ref[n]
        dkv[n] = jnp.zeros((128, SUPER), jnp.float32)

    rel = lax.broadcasted_iota(jnp.int32, (ROWS, SUPER), 0) - lax.broadcasted_iota(
        jnp.int32, (ROWS, SUPER), 1
    )

    table[pl.ds(0, ROWS), :] = jnp.full((ROWS, SUPER), LOW, jnp.float32)
    for c in range(2):
        d = rel + (SUPER * c + ROWS * x)
        value = jnp.full((ROWS, SUPER), LOW, jnp.float32)
        for k in range(8):
            value = jnp.where(d >= k, rab_ref[k] * 0.5, value)
        for p in range(3, 10):
            value = jnp.where(d >= 2**p, rab_ref[p + 6] * 0.5, value)
        table[pl.ds((c + 1) * ROWS, ROWS), :] = value

    @pl.loop(2, CLASSES - 1)
    def _(c):
        base = SUPER * c + ROWS * x
        lowest = base - (SUPER - 1)
        b = bucket_scalar(lowest)
        d = rel + base
        value = jnp.where(
            d >= next_power(lowest), rab_ref[jnp.minimum(b + 1, NB - 1)] * 0.5, rab_ref[b] * 0.5
        )
        table[pl.ds(pl.multiple_of((c + 1) * ROWS, ROWS), ROWS), :] = value

    @pl.loop(0, CLASSES)
    def _(c):
        biasacc[pl.ds(pl.multiple_of(c * ROWS, ROWS), ROWS), :] = jnp.zeros(
            (ROWS, SUPER), jnp.float32
        )

    lane = lax.broadcasted_iota(jnp.int32, (2 * ROWS, 128), 1)
    left = lane < HD

    def start_of(pos):
        start = jnp.int32(0)
        for d in range(1, DOCS):
            start = jnp.where(pos >= bounds_ref[d], bounds_ref[d], start)
        return start

    @pl.loop(0, GROUPS)
    def _(g):
        row = lax.broadcasted_iota(jnp.int32, (2 * ROWS, 128), 0)
        pos = 2 * SUPER * g + ROWS * x + row + jnp.where(row >= ROWS, SUPER - ROWS, 0)
        start = jnp.zeros((2 * ROWS, 128), jnp.int32)
        length = jnp.zeros((2 * ROWS, 128), jnp.int32)
        for d in range(DOCS):
            first = bounds_ref[d]
            end = bounds_ref[d + 1] if d + 1 < DOCS else jnp.int32(2 * SUPER * GROUPS)
            inside = pos >= first
            start = jnp.where(inside, first, start)
            length = jnp.where(inside, end - first, length)
        start_ref[...] = start
        scale_ref[...] = lax.rsqrt(length.astype(jnp.float32))
        qg = qs[g]
        zero = jnp.zeros_like(qg)
        lhs[pl.ds(0, 2 * ROWS), :] = jnp.where(left, qg, zero)
        lhs[pl.ds(2 * ROWS, 2 * ROWS), :] = jnp.where(left, zero, qg)
        qgt[...] = qg.T
        acc[...] = jnp.zeros((2 * ROWS, 128), jnp.float32)
        first_pos = 2 * SUPER * g + ROWS * x
        start_first = start_of(first_pos)
        start_last = start_of(first_pos + SUPER + ROWS - 1)
        low = lax.div(lax.div(start_first, SUPER) - core + 1, 2)

        def tile(n, masked):
            mk = 2 * n + core
            at = pl.multiple_of((2 * g - mk + 1) * ROWS, ROWS)
            keyvals = kvs[n]
            both = lax.dot_general(lhs[...], keyvals, NT, preferred_element_type=jnp.float32)
            half = both[: 2 * ROWS] + table[pl.ds(at, 2 * ROWS), :]
            if masked:
                key = SUPER * mk + lax.broadcasted_iota(jnp.int32, (2 * ROWS, SUPER), 1)
                starts = jnp.concatenate([start_ref[...]] * 3, axis=1)
                half = jnp.where(key >= starts, half, LOW)
            t = jnp.tanh(half)
            u = 1.0 + t
            w = half * u
            ds = both[2 * ROWS :] * (u + w * (1.0 - t))
            biasacc[pl.ds(at, 2 * ROWS), :] += ds
            wb = w.astype(jnp.bfloat16)
            db = ds.astype(jnp.bfloat16)
            od = jnp.dot(
                jnp.concatenate([wb, db], axis=0), keyvals, preferred_element_type=jnp.float32
            )
            acc[...] += jnp.where(left, od[2 * ROWS :], od[: 2 * ROWS])
            dkv[n, pl.ds(0, HD), :] += jnp.dot(
                qgt[pl.ds(0, HD), :], db, preferred_element_type=jnp.float32
            )
            dkv[n, pl.ds(HD, HD), :] += jnp.dot(
                qgt[pl.ds(HD, HD), :], wb, preferred_element_type=jnp.float32
            )

        @pl.loop(low, g + 1)
        def _(n):
            clear = SUPER * (2 * n + core) >= start_last

            @pl.when(clear)
            def _():
                tile(n, False)

            @pl.when(jnp.logical_not(clear))
            def _():
                tile(n, True)

        result = acc[...] * jnp.where(left, 0.0625, scale_ref[...])
        acc[...] = result
        mine_ref[g] = acc[pl.ds(mine_at, ROWS), :]
        theirs_ref[g] = acc[pl.ds(theirs_at, ROWS), :].astype(jnp.bfloat16)

    @pl.loop(0, GROUPS)
    def _(n):
        kvs[n] = dkv[n].astype(jnp.bfloat16).T

    for r, ref in enumerate((d0, d1, d2, d3)):
        at = pl.multiple_of(lax.rem(x + r, 4) * ROWS, ROWS)

        @pl.loop(0, GROUPS)
        def _(n):
            ref[n] = kvs[n, pl.ds(at, ROWS), :]

    buckets[...] = jnp.zeros((NB, 8, 128), jnp.float32)

    def fold(v):
        v = v[:, :128] + v[:, 128:256] + v[:, 256:]
        out = v[:8]
        for i in range(1, ROWS // 8):
            out = out + v[8 * i : 8 * i + 8]
        return out

    for c in range(2):
        d = rel + (SUPER * c + ROWS * x)
        v = biasacc[pl.ds((c + 1) * ROWS, ROWS), :]
        edges = [(k, k, k + 1) for k in range(8)] + [(p + 6, 2**p, 2 ** (p + 1)) for p in range(3, 10)]
        for b, first, end in edges:
            buckets[b] += fold(jnp.where((d >= first) & (d < end), v, 0.0))

    @pl.loop(2, CLASSES - 1)
    def _(c):
        base = SUPER * c + ROWS * x
        lowest = base - (SUPER - 1)
        b = bucket_scalar(lowest)
        d = rel + base
        v = biasacc[pl.ds(pl.multiple_of((c + 1) * ROWS, ROWS), ROWS), :]
        upper = d >= next_power(lowest)
        buckets[b] += fold(jnp.where(upper, 0.0, v))
        buckets[jnp.minimum(b + 1, NB - 1)] += fold(jnp.where(upper, v, 0.0))

    for b in range(NB):
        bias_ref[pl.ds(b, 1), :] = jnp.sum(buckets[b], axis=0, keepdims=True) * 0.5


def unpack_kernel(qo_ref, dkv_ref, out_ref, grad_ref):
    for h in range(0, H, 2):
        cols = slice(h * HD, (h + 2) * HD)
        a, b = qo_ref[h], qo_ref[h + 1]
        grad_ref[:, 0, cols] = jnp.concatenate([a[:, :HD], b[:, :HD]], axis=1)
        out_ref[:, cols] = jnp.concatenate([a[:, HD:], b[:, HD:]], axis=1)
        a, b = dkv_ref[h, :ROWS], dkv_ref[h + 1, :ROWS]
        grad_ref[:, 1, cols] = jnp.concatenate([a[:, :HD], b[:, :HD]], axis=1)
        grad_ref[:, 2, cols] = jnp.concatenate([a[:, HD:], b[:, HD:]], axis=1)


def shift(v, axis, n, by):
    return lax.ppermute(v, axis, [(i, (i + by) % n) for i in range(n)])


def per_device(qkv, grad_out, rab, doc_ids):
    bf16, f32 = jnp.bfloat16, jnp.float32
    x, y, z, core = (lax.axis_index(a) for a in ("x", "y", "z", "core"))
    whole = pl.BlockSpec(memory_space=VMEM)
    scalars = pl.BlockSpec(memory_space=SMEM)
    block = jax.ShapeDtypeStruct((H, ROWS, 128), bf16)
    params = pltpu.CompilerParams(vmem_limit_bytes=48 * 2**20)
    first_row = (((y * 4 + z) * 2 + core) * 4 + x) * ROWS
    kv, qg, bounds = pl.pallas_call(
        pack_kernel,
        out_shape=(block, block, jax.ShapeDtypeStruct((DOCS,), jnp.int32)),
        in_specs=[scalars, whole, whole, whole],
        out_specs=(whole, whole, scalars),
        compiler_params=params,
        name="pack",
    )(first_row.reshape(1), doc_ids.reshape(96, 128), qkv, grad_out)
    kv = lax.all_to_all(kv, ("y", "z"), 0, 0, tiled=True)
    kvs = [kv] + [shift(kv, "x", 4, -r) for r in (1, 2, 3)]
    qg = lax.all_to_all(qg, ("y", "z"), 0, 0, tiled=True)
    qg_other = shift(qg, "core", 2, 1)
    table_row = lax.dynamic_slice_in_dim(rab, y * 4 + z, 1, 0)[0]
    d0, d1, d2, d3, mine, theirs, bias = pl.pallas_call(
        main_kernel,
        out_shape=(
            [block] * 4
            + [
                jax.ShapeDtypeStruct((H, ROWS, 128), f32),
                block,
                jax.ShapeDtypeStruct((NB, 128), f32),
            ]
        ),
        in_specs=[scalars] * 3 + [whole] * 6,
        out_specs=[whole] * 7,
        scratch_shapes=[
            VMEM((GROUPS, SUPER, 128), bf16),
            VMEM((GROUPS, 2 * ROWS, 128), bf16),
            VMEM((CLASSES * ROWS, SUPER), f32),
            VMEM((CLASSES * ROWS, SUPER), f32),
            VMEM((GROUPS, 128, SUPER), f32),
            VMEM((2 * ROWS, 128), jnp.int32),
            VMEM((2 * ROWS, 128), f32),
            VMEM((2 * ROWS, 128), f32),
            VMEM((4 * ROWS, 128), bf16),
            VMEM((128, 2 * ROWS), bf16),
            VMEM((NB, 8, 128), f32),
        ],
        compiler_params=params,
        name="attend",
    )(jnp.stack([x, core]), bounds, table_row, *kvs, qg, qg_other)
    parts = [shift(d, "x", 4, r) for r, d in ((1, d1), (2, d2), (3, d3))]
    theirs = shift(theirs, "core", 2, 1)
    bias = jnp.sum(bias, axis=1)
    bias = bias + shift(bias, "core", 2, 1)
    bias = bias + shift(bias, "x", 4, 1)
    bias = bias + shift(bias, "x", 4, 2)
    hi = lax.reduce_precision(bias, 8, 7)
    mid = lax.reduce_precision(bias - hi, 8, 7)
    lo = bias - hi - mid
    carried = jnp.pad(jnp.stack([hi, mid, lo]).astype(bf16), ((0, 13), (0, 128 - NB)))
    qo = (mine + theirs.astype(f32)).astype(bf16)
    dkv = d0.astype(f32) + parts[0].astype(f32) + parts[1].astype(f32) + parts[2].astype(f32)
    dkv = jnp.concatenate(
        [dkv.astype(bf16), jnp.broadcast_to(carried[None], (H, 16, 128))], axis=1
    )
    qo = lax.all_to_all(qo, ("y", "z"), 0, 0, tiled=True)
    dkv = lax.all_to_all(dkv, ("y", "z"), 0, 0, tiled=True)
    terms = lax.dynamic_slice(dkv, (x * 4, ROWS, 0), (4, 3, NB)).astype(f32)
    bias_grad = terms[:, 0] + terms[:, 1] + terms[:, 2]
    out, grad_qkv = pl.pallas_call(
        unpack_kernel,
        out_shape=(
            jax.ShapeDtypeStruct((ROWS, H * HD), bf16),
            jax.ShapeDtypeStruct((ROWS, 3, H * HD), bf16),
        ),
        in_specs=[whole, whole],
        out_specs=(whole, whole),
        compiler_params=params,
        name="unpack",
    )(qo, dkv)
    return out, grad_qkv, bias_grad


def solution(mesh):
    fine = Mesh(mesh.devices.reshape(4, 4, 4, 2), ("x", "y", "z", "core"))
    rows = ("y", "z", "core", "x")
    return jax.shard_map(
        per_device,
        mesh=fine,
        in_specs=(P(rows, None, None), P(rows, None), P(), P()),
        out_specs=(P(rows, None), P(rows, None, None), P("x", None)),
        check_vma=False,
    )
```

```python
import jax
import jax.numpy as jnp
from jax import lax
from jax.experimental import pallas as pl
from jax.experimental.pallas import tpu as pltpu
from jax.sharding import Mesh
from jax.sharding import PartitionSpec as P

HD = 64
H = 16
NB = 20
DOCS = 8
ROWS = 96
SUPER = 384
GROUPS = 16
PAIR = 768
TALL = 192
WIDE = 256
SLOTS = 256
DEPTH = 6
LOW = -1e30
VMEM = pltpu.VMEM
SMEM = pltpu.SMEM
NT = (((1,), (1,)), ((), ()))


def doc_bounds(ids):
    return [jnp.int32(0)] + [
        jnp.sum((ids < d).astype(jnp.float32)).astype(jnp.int32) for d in range(1, DOCS)
    ]


def pack_kernel(where_ref, ids_ref, qkv_ref, g_ref, out_ref, bounds_ref):
    bounds = doc_bounds(ids_ref[...])
    for d in range(DOCS):
        bounds_ref[d] = bounds[d]
    pos = where_ref[0] + lax.broadcasted_iota(jnp.int32, (ROWS, 128), 0)
    length = jnp.zeros((ROWS, 128), jnp.int32)
    ends = bounds[1:] + [jnp.int32(PAIR * GROUPS)]
    for d in range(DOCS):
        length = jnp.where(pos >= bounds[d], ends[d] - bounds[d], length)
    scale = lax.rsqrt(length.astype(jnp.float32))[:, :HD]
    for h in range(H):
        cols = slice(h * HD, (h + 1) * HD)
        out_ref[h, :ROWS] = jnp.concatenate([qkv_ref[1, :, cols], qkv_ref[2, :, cols]], axis=1)
        q = (qkv_ref[0, :, cols].astype(jnp.float32) * 0.0625).astype(jnp.bfloat16)
        g = (g_ref[:, cols].astype(jnp.float32) * scale).astype(jnp.bfloat16)
        out_ref[h, ROWS:] = jnp.concatenate([q, g], axis=1)


EDGES = [(k, k) for k in range(8)] + [(2**p, p + 6) for p in range(3, 13)]


def edges_of(low, high):
    below = [edge for edge in EDGES if edge[0] <= low]
    return below[-1:], [edge for edge in EDGES if low < edge[0] <= high]


def key_lanes(x, j, second):
    if second:
        late = j >= 128
        j = j + jnp.where(late, 128, 256)
    place = j + 2 * ROWS * lax.div(x, 2) + jnp.where(j >= 2 * ROWS, SUPER - 2 * ROWS, 0)
    return place + jnp.where(late, PAIR, 0) if second else place


SLABS = [
    (PAIR * e - (1535 if second else 639), PAIR * e + (319 if second else 767), e, second)
    for second, count in ((False, 9), (True, 10))
    for e in range(count)
]


def distance(x, core, e, second, row):
    i = row + lax.broadcasted_iota(jnp.int32, (16, WIDE), 0)
    j = lax.broadcasted_iota(jnp.int32, (16, WIDE), 1)
    lower = jnp.minimum(x, 3 - x)
    i = i + ROWS * lower + jnp.where(i >= ROWS, ROWS * (2 - 2 * lower), 0)
    return PAIR * e + SUPER * core + i - key_lanes(x, j, second)


def start_of(bounds_ref, pos):
    start = jnp.int32(0)
    for d in range(1, DOCS):
        start = jnp.where(pos >= bounds_ref[d], bounds_ref[d], start)
    return start


def span_of(x, core, g):
    lower = jnp.minimum(x, 3 - x)
    base = PAIR * g + SUPER * core
    return base + ROWS * lower, base + ROWS * (4 - lower) - 1


def table_kernel(where_ref, rab_ref, bounds_ref, table_ref, plan_ref):
    x, core = where_ref[0], where_ref[1]

    def put(at, g, tile, slab):
        plan_ref[at] = g
        plan_ref[SLOTS + at] = tile
        plan_ref[2 * SLOTS + at] = slab

    put(0, 0, 0, 0)

    def of_group(g, count):
        low = lax.div(start_of(bounds_ref, span_of(x, core, g)[0]), PAIR)

        def first(n, count):
            m = lax.div(n, 2)
            put(count + 1, g, m + n, g - n + 1)
            return count + 1

        def second(m, count):
            put(count + 1, g, 3 * m + 2, g - 2 * m + 10)
            return count + 1

        count = lax.fori_loop(low, g + 1, first, count)
        return lax.fori_loop(lax.div(low, 2), lax.div(g + core + 1, 2), second, count)

    count = lax.fori_loop(0, GROUPS, of_group, jnp.int32(0))
    plan_ref[3 * SLOTS] = count
    for extra in range(1, DEPTH + 2):
        put(count + extra, 0, 0, 0)
    table_ref[0] = jnp.full((TALL, WIDE), LOW, jnp.float32)
    for index, (low, high, e, second) in enumerate(SLABS):
        below, inside = edges_of(low, high)

        @pl.loop(0, TALL // 16)
        def _(step):
            row = pl.multiple_of(step * 16, 16)
            d = distance(x, core, e, second, row)
            value = jnp.full((16, WIDE), rab_ref[below[0][1]] * 0.5 if below else LOW, jnp.float32)
            for edge, b in inside:
                value = jnp.where(d >= edge, rab_ref[b] * 0.5, value)
            table_ref[index + 1, pl.ds(row, 16), :] = value


def buckets_kernel(where_ref, sums_ref, bias_ref, buckets):
    x, core = where_ref[0], where_ref[1]
    buckets[...] = jnp.zeros((NB, 8, 128), jnp.float32)

    def fold(v):
        v = v[:, :128] + v[:, 128:]
        return v[:8] + v[8:]

    for index, (low, high, e, second) in enumerate(SLABS):
        below, inside = edges_of(low, high)

        def step(k, carry):
            row = pl.multiple_of(k * 16, 16)
            d = distance(x, core, e, second, row)
            v = sums_ref[index + 1, pl.ds(row, 16), :]
            terms = [fold(v)] if below else []
            terms = terms + [fold(jnp.where(d >= edge, v, 0.0)) for edge, b in inside]
            return tuple(c + t for c, t in zip(carry, terms))

        found = below + inside
        zero = jnp.zeros((8, 128), jnp.float32)
        sums = lax.fori_loop(0, TALL // 16, step, (zero,) * len(found))
        for k, (edge, b) in enumerate(found):
            rest = sums[k + 1] if k + 1 < len(found) else zero
            buckets[b] += sums[k] - rest
    lane = lax.broadcasted_iota(jnp.int32, (8, 128), 1)
    row = jnp.zeros((8, 128), jnp.float32)
    for b in range(NB):
        total = jnp.sum(jnp.sum(buckets[b], axis=0, keepdims=True), axis=1, keepdims=True)
        row = jnp.where(lane == b, total * 0.5, row)
    bias_ref[...] = row


def main_kernel(
    where_ref, bounds_ref, plan_ref, table, own_ref, kvx_ref, kvc_ref, kvxc_ref, qgx_ref,
    keep_ref, give_ref, mine_ref, theirs_ref, biasacc,
    line, kvs, dkv, starts, scales, acc, lhs, qgt, *stages,
):
    x = where_ref[0]
    core = where_ref[1]
    odd = lax.rem(x, 2)
    lower = jnp.minimum(x, 3 - x)

    def aligned(v):
        return pl.multiple_of(v * ROWS, ROWS)

    k_own = aligned(2 * core + odd)
    k_x = aligned(2 * core + 1 - odd)
    k_core = aligned(2 * (1 - core) + odd)
    k_both = aligned(2 * (1 - core) + 1 - odd)
    q_own = aligned((x != lower).astype(jnp.int32))
    q_x = aligned((x == lower).astype(jnp.int32))
    lane = lax.broadcasted_iota(jnp.int32, (TALL, 128), 1)
    left = lane < HD
    row = lax.broadcasted_iota(jnp.int32, (TALL, 128), 0)
    offset = row + jnp.where(row >= ROWS, ROWS * (2 - 2 * lower), 0)

    @pl.loop(0, GROUPS)
    def _(n):
        line[n, pl.ds(k_own, ROWS), :] = own_ref[n, :ROWS]
        line[n, pl.ds(k_x, ROWS), :] = kvx_ref[n]
        line[n, pl.ds(k_core, ROWS), :] = kvc_ref[n]
        line[n, pl.ds(k_both, ROWS), :] = kvxc_ref[n]
        acc[n] = jnp.zeros((TALL, 128), jnp.float32)
        zero = jnp.zeros((ROWS, 128), jnp.bfloat16)
        for at, qg in ((q_own, own_ref[n, ROWS:]), (q_x, qgx_ref[n])):
            lhs[n, pl.ds(at, ROWS), :] = jnp.where(left[:ROWS], qg, zero)
            lhs[n, pl.ds(pl.multiple_of(at + TALL, ROWS), ROWS), :] = jnp.where(left[:ROWS], zero, qg)
        qgt[n] = (lhs[n, pl.ds(0, TALL), :] + lhs[n, pl.ds(TALL, TALL), :]).T
        first, last = span_of(x, core, n)
        pos = first + offset

        def history(d, low):
            begin = bounds_ref[d]
            end = jnp.where(d + 1 < DOCS, bounds_ref[jnp.minimum(d + 1, DOCS - 1)], PAIR * GROUPS)
            inside = pos >= begin
            size = jnp.full((TALL, 128), end - begin, jnp.int32).astype(jnp.float32)
            starts[n] = jnp.where(inside, begin, starts[n])
            scales[n] = jnp.where(left, 0.0625, jnp.where(inside, lax.rsqrt(size), scales[n]))
            return low

        d_first, d_last = jnp.int32(0), jnp.int32(0)
        for d in range(1, DOCS):
            d_first = d_first + (first >= bounds_ref[d]).astype(jnp.int32)
            d_last = d_last + (last >= bounds_ref[d]).astype(jnp.int32)
        starts[n] = jnp.zeros((TALL, 128), jnp.int32)
        scales[n] = jnp.zeros((TALL, 128), jnp.float32)
        lax.fori_loop(d_first, d_last + 1, history, 0)

    @pl.loop(0, GROUPS // 2)
    def _(m):
        kvs[3 * m] = line[2 * m, :WIDE]
        kvs[3 * m + 1] = line[2 * m + 1, :WIDE]
        kvs[3 * m + 2, :128] = line[2 * m, WIDE:]
        kvs[3 * m + 2, 128:] = line[2 * m + 1, WIDE:]
        for r in range(3):
            dkv[3 * m + r] = jnp.zeros((128, WIDE), jnp.float32)

    @pl.loop(0, len(SLABS) + 1)
    def _(e):
        biasacc[e] = jnp.zeros((TALL, WIDE), jnp.float32)

    score, weight = stages[:DEPTH], stages[DEPTH:]
    weight[0][...] = jnp.zeros((2 * TALL, WIDE), jnp.bfloat16)
    j = lax.broadcasted_iota(jnp.int32, (1, WIDE), 1)
    first_lanes, second_lanes = key_lanes(x, j, False), key_lanes(x, j, True)

    def scores(k, s):
        g, n = plan_ref[k], plan_ref[SLOTS + k]
        s[...] = lax.dot_general(lhs[g], kvs[n], NT, preferred_element_type=jnp.float32)

    def weigh(k, s, w_out):
        g, n, e = plan_ref[k], plan_ref[SLOTS + k], plan_ref[2 * SLOTS + k]
        m = lax.div(n, 3)
        key = jnp.where(e > 9, second_lanes, first_lanes)
        key = key + PAIR * (2 * m + (n - 3 * m == 1).astype(jnp.int32))
        begin = jnp.concatenate([starts[g]] * 2, axis=1)
        half = jnp.where(key >= begin, s[pl.ds(0, TALL), :] + table[e], LOW)
        t = jnp.tanh(half)
        u = 1.0 + t
        w = half * u
        ds = s[pl.ds(TALL, TALL), :] * (u + w * (1.0 - t))
        biasacc[e] += ds
        w_out[pl.ds(0, TALL), :] = w.astype(jnp.bfloat16)
        w_out[pl.ds(TALL, TALL), :] = ds.astype(jnp.bfloat16)

    def gather(k, w_in):
        g, n = plan_ref[k], plan_ref[SLOTS + k]
        od = jnp.dot(w_in[...], kvs[n], preferred_element_type=jnp.float32)
        acc[g] += jnp.where(left, od[TALL:], od[:TALL])
        dkv[n, pl.ds(0, HD), :] += jnp.dot(
            qgt[g, pl.ds(0, HD), :], w_in[pl.ds(TALL, TALL), :], preferred_element_type=jnp.float32
        )
        dkv[n, pl.ds(HD, HD), :] += jnp.dot(
            qgt[g, pl.ds(HD, HD), :], w_in[pl.ds(0, TALL), :], preferred_element_type=jnp.float32
        )

    scores(1, score[1])

    @pl.loop(0, lax.div(plan_ref[3 * SLOTS] + DEPTH, DEPTH))
    def _(step):
        for i in range(DEPTH):
            k = DEPTH * step + i
            now, later = (i + 1) % DEPTH, (i + 2) % DEPTH
            gather(k, weight[i])
            weigh(k + 1, score[now], weight[now])
            scores(k + 2, score[later])

    @pl.loop(0, GROUPS // 2)
    def _(m):
        line[2 * m, :WIDE] = dkv[3 * m].astype(jnp.bfloat16).T
        line[2 * m + 1, :WIDE] = dkv[3 * m + 1].astype(jnp.bfloat16).T
        last = dkv[3 * m + 2].astype(jnp.bfloat16).T
        line[2 * m, WIDE:] = last[:128]
        line[2 * m + 1, WIDE:] = last[128:]

    @pl.loop(0, GROUPS)
    def _(n):
        acc[n] = acc[n] * scales[n]
        mine_ref[n] = acc[n, pl.ds(q_own, ROWS), :]
        theirs_ref[n] = acc[n, pl.ds(q_x, ROWS), :].astype(jnp.bfloat16)
        keep_ref[n, :ROWS] = line[n, pl.ds(k_own, ROWS), :]
        keep_ref[n, ROWS:] = line[n, pl.ds(k_x, ROWS), :]
        give_ref[n, :ROWS] = line[n, pl.ds(k_core, ROWS), :]
        give_ref[n, ROWS:] = line[n, pl.ds(k_both, ROWS), :]


def unpack_kernel(in_ref, out_ref, grad_ref):
    for h in range(0, H, 2):
        cols = slice(h * HD, (h + 2) * HD)
        a, b = in_ref[h, :ROWS], in_ref[h + 1, :ROWS]
        grad_ref[0, :, cols] = jnp.concatenate([a[:, :HD], b[:, :HD]], axis=1)
        out_ref[:, cols] = jnp.concatenate([a[:, HD:], b[:, HD:]], axis=1)
        a, b = in_ref[h, ROWS : 2 * ROWS], in_ref[h + 1, ROWS : 2 * ROWS]
        grad_ref[1, :, cols] = jnp.concatenate([a[:, :HD], b[:, :HD]], axis=1)
        grad_ref[2, :, cols] = jnp.concatenate([a[:, HD:], b[:, HD:]], axis=1)


def swap(v, axis, partner):
    return lax.ppermute(v, axis, [(i, p) for i, p in enumerate(partner)])


def per_device(qkv, grad_out, rab, doc_ids):
    bf16, f32 = jnp.bfloat16, jnp.float32
    x, y, z, core = (lax.axis_index(a) for a in ("x", "y", "z", "core"))
    whole = pl.BlockSpec(memory_space=VMEM)
    scalars = pl.BlockSpec(memory_space=SMEM)
    block = jax.ShapeDtypeStruct((H, ROWS, 128), bf16)
    double = jax.ShapeDtypeStruct((H, 2 * ROWS, 128), bf16)
    slabs = jax.ShapeDtypeStruct((len(SLABS) + 1, TALL, WIDE), f32)
    params = pltpu.CompilerParams(vmem_limit_bytes=48 * 2**20)
    first_row = (((y * 4 + z) * 2 + core) * 4 + x) * ROWS
    where = jnp.stack([x, core])
    packed, bounds = pl.pallas_call(
        pack_kernel,
        out_shape=(double, jax.ShapeDtypeStruct((DOCS,), jnp.int32)),
        in_specs=[scalars, whole, whole, whole],
        out_specs=(whole, scalars),
        compiler_params=params,
        name="pack",
    )(first_row.reshape(1), doc_ids.reshape(96, 128), qkv.transpose(1, 0, 2), grad_out)
    own = lax.all_to_all(packed, ("y", "z"), 0, 0, tiled=True)
    kv_own, qg_own = own[:, :ROWS], own[:, ROWS:]
    kv_x = swap(kv_own, "x", (1, 0, 3, 2))
    qg_x = swap(qg_own, "x", (3, 2, 1, 0))
    kv_core = swap(kv_own, "core", (1, 0))
    kv_both = swap(kv_x, "core", (1, 0))
    table_row = lax.dynamic_slice_in_dim(rab, y * 4 + z, 1, 0)[0]
    table, plan = pl.pallas_call(
        table_kernel,
        out_shape=(slabs, jax.ShapeDtypeStruct((3 * SLOTS + 1,), jnp.int32)),
        in_specs=[scalars] * 3,
        out_specs=(whole, scalars),
        compiler_params=params,
        cost_estimate=pl.CostEstimate(flops=10**7, bytes_accessed=3 * 10**6, transcendentals=0),
        name="table",
    )(where, table_row, bounds)
    keep, give, mine, theirs, sums = pl.pallas_call(
        main_kernel,
        out_shape=[double, double, jax.ShapeDtypeStruct((H, ROWS, 128), f32), block, slabs],
        in_specs=[scalars] * 3 + [whole] * 6,
        out_specs=[whole] * 5,
        scratch_shapes=[
            VMEM((GROUPS, SUPER, 128), bf16),
            VMEM((24, WIDE, 128), bf16),
            VMEM((24, 128, WIDE), f32),
            VMEM((GROUPS, TALL, 128), jnp.int32),
            VMEM((GROUPS, TALL, 128), f32),
            VMEM((GROUPS, TALL, 128), f32),
            VMEM((GROUPS, 2 * TALL, 128), bf16),
            VMEM((GROUPS, 128, TALL), bf16),
        ]
        + [VMEM((2 * TALL, WIDE), f32)] * DEPTH
        + [VMEM((2 * TALL, WIDE), bf16)] * DEPTH,
        compiler_params=params,
        name="attend",
    )(where, bounds, plan, table, own, kv_x, kv_core, kv_both, qg_x)
    got = swap(give, "core", (1, 0))
    got_qo = swap(theirs, "x", (3, 2, 1, 0))
    bias = pl.pallas_call(
        buckets_kernel,
        out_shape=jax.ShapeDtypeStruct((8, 128), f32),
        in_specs=[scalars, whole],
        out_specs=whole,
        scratch_shapes=[VMEM((NB, 8, 128), f32)],
        compiler_params=params,
        cost_estimate=pl.CostEstimate(flops=10**7, bytes_accessed=3 * 10**6, transcendentals=0),
        name="buckets",
    )(where, sums)
    dkv = keep.astype(f32) + got.astype(f32)
    got_dkv = swap(dkv[:, ROWS:].astype(bf16), "x", (1, 0, 3, 2))
    bias = bias + swap(bias, "core", (1, 0))
    bias = bias + sum(swap(bias, "x", p) for p in ((1, 0, 3, 2), (3, 2, 1, 0), (2, 3, 0, 1)))
    bias = bias[0]
    hi = lax.reduce_precision(bias, 8, 7)
    mid = lax.reduce_precision(bias - hi, 8, 7)
    lo = bias - hi - mid
    carried = jnp.pad(jnp.stack([hi, mid, lo]).astype(bf16), ((0, 13), (0, 0)))
    results = jnp.concatenate(
        [
            (mine + got_qo.astype(f32)).astype(bf16),
            (dkv[:, :ROWS] + got_dkv.astype(f32)).astype(bf16),
            jnp.broadcast_to(carried[None], (H, 16, 128)),
        ],
        axis=1,
    )
    results = lax.all_to_all(results, ("y", "z"), 0, 0, tiled=True)
    terms = lax.dynamic_slice(results, (x * 4, 2 * ROWS, 0), (4, 3, NB)).astype(f32)
    bias_grad = terms[:, 0] + terms[:, 1] + terms[:, 2]
    out, grad_qkv = pl.pallas_call(
        unpack_kernel,
        out_shape=(
            jax.ShapeDtypeStruct((ROWS, H * HD), bf16),
            jax.ShapeDtypeStruct((3, ROWS, H * HD), bf16),
        ),
        in_specs=[whole],
        out_specs=(whole, whole),
        compiler_params=params,
        name="unpack",
    )(results)
    return out, grad_qkv.transpose(1, 0, 2), bias_grad


def solution(mesh):
    fine = Mesh(mesh.devices.reshape(4, 4, 4, 2), ("x", "y", "z", "core"))
    rows = ("y", "z", "core", "x")
    return jax.shard_map(
        per_device,
        mesh=fine,
        in_specs=(P(rows, None, None), P(rows, None), P(), P()),
        out_specs=(P(rows, None), P(rows, None, None), P("x", None)),
        check_vma=False,
    )
```

```python
import jax
import jax.numpy as jnp
from jax import lax
from jax.experimental import pallas as pl
from jax.experimental.pallas import tpu as pltpu
from jax.sharding import Mesh
from jax.sharding import PartitionSpec as P

HD = 64
H = 16
NB = 20
DOCS = 8
ROWS = 96
SUPER = 384
GROUPS = 16
PAIR = 768
TALL = 192
WIDE = 256
SLOTS = 256
DEPTH = 6
LOW = -1e30
VMEM = pltpu.VMEM
SMEM = pltpu.SMEM
NT = (((1,), (1,)), ((), ()))


def doc_bounds(ids):
    return [jnp.int32(0)] + [
        jnp.sum((ids < d).astype(jnp.float32)).astype(jnp.int32) for d in range(1, DOCS)
    ]


def pack_kernel(where_ref, ids_ref, qkv_ref, g_ref, out_ref, bounds_ref):
    bounds = doc_bounds(ids_ref[...])
    for d in range(DOCS):
        bounds_ref[d] = bounds[d]
    pos = where_ref[0] + lax.broadcasted_iota(jnp.int32, (ROWS, 128), 0)
    length = jnp.zeros((ROWS, 128), jnp.int32)
    ends = bounds[1:] + [jnp.int32(PAIR * GROUPS)]
    for d in range(DOCS):
        length = jnp.where(pos >= bounds[d], ends[d] - bounds[d], length)
    scale = lax.rsqrt(length.astype(jnp.float32))[:, :HD]
    for h in range(H):
        cols = slice(h * HD, (h + 1) * HD)
        out_ref[h, :ROWS] = jnp.concatenate([qkv_ref[1, :, cols], qkv_ref[2, :, cols]], axis=1)
        q = (qkv_ref[0, :, cols].astype(jnp.float32) * 0.0625).astype(jnp.bfloat16)
        g = (g_ref[:, cols].astype(jnp.float32) * scale).astype(jnp.bfloat16)
        out_ref[h, ROWS:] = jnp.concatenate([q, g], axis=1)


EDGES = [(k, k) for k in range(8)] + [(2**p, p + 6) for p in range(3, 13)]


def edges_of(low, high):
    below = [edge for edge in EDGES if edge[0] <= low]
    return below[-1:], [edge for edge in EDGES if low < edge[0] <= high]


def key_lanes(x, j, second):
    if second:
        late = j >= 128
        j = j + jnp.where(late, 128, 256)
    place = j + 2 * ROWS * lax.div(x, 2) + jnp.where(j >= 2 * ROWS, SUPER - 2 * ROWS, 0)
    return place + jnp.where(late, PAIR, 0) if second else place


SLABS = [
    (PAIR * e - (1535 if second else 639), PAIR * e + (319 if second else 767), e, second)
    for second, count in ((False, 9), (True, 10))
    for e in range(count)
]


def distance(x, core, second, row):
    i = row + lax.broadcasted_iota(jnp.int32, (16, WIDE), 0)
    j = lax.broadcasted_iota(jnp.int32, (16, WIDE), 1)
    lower = jnp.minimum(x, 3 - x)
    i = i + ROWS * lower + jnp.where(i >= ROWS, ROWS * (2 - 2 * lower), 0)
    return SUPER * core + i - key_lanes(x, j, second)


def start_of(bounds_ref, pos):
    start = jnp.int32(0)
    for d in range(1, DOCS):
        start = jnp.where(pos >= bounds_ref[d], bounds_ref[d], start)
    return start


def span_of(x, core, g):
    lower = jnp.minimum(x, 3 - x)
    base = PAIR * g + SUPER * core
    return base + ROWS * lower, base + ROWS * (4 - lower) - 1


def table_kernel(where_ref, rab_ref, bounds_ref, table_ref, plan_ref):
    x, core = where_ref[0], where_ref[1]

    def put(at, g, tile, slab):
        plan_ref[at] = g
        plan_ref[SLOTS + at] = tile
        plan_ref[2 * SLOTS + at] = slab

    put(0, 0, 0, 0)

    def of_group(g, count):
        low = lax.div(start_of(bounds_ref, span_of(x, core, g)[0]), PAIR)

        def first(n, count):
            m = lax.div(n, 2)
            put(count + 1, g, m + n, g - n + 1)
            return count + 1

        def second(m, count):
            put(count + 1, g, 3 * m + 2, g - 2 * m + 10)
            return count + 1

        count = lax.fori_loop(low, g + 1, first, count)
        return lax.fori_loop(lax.div(low, 2), lax.div(g + core + 1, 2), second, count)

    count = lax.fori_loop(0, GROUPS, of_group, jnp.int32(0))
    plan_ref[3 * SLOTS] = count
    for extra in range(1, DEPTH + 2):
        put(count + extra, 0, 0, 0)
    table_ref[0] = jnp.full((TALL, WIDE), LOW, jnp.float32)

    @pl.loop(0, TALL // 16)
    def _(step):
        row = pl.multiple_of(step * 16, 16)
        near = [distance(x, core, second, row) for second in (False, True)]
        for index, (low, high, e, second) in enumerate(SLABS):
            below, inside = edges_of(low, high)
            value = jnp.full((16, WIDE), rab_ref[below[0][1]] * 0.5 if below else LOW, jnp.float32)
            for edge, b in inside:
                value = jnp.where(near[second] >= edge - PAIR * e, rab_ref[b] * 0.5, value)
            table_ref[index + 1, pl.ds(row, 16), :] = value


def buckets_kernel(where_ref, sums_ref, bias_ref, buckets):
    x, core = where_ref[0], where_ref[1]
    buckets[...] = jnp.zeros((NB, 8, 128), jnp.float32)

    def fold(v):
        v = v[:, :128] + v[:, 128:]
        return v[:8] + v[8:]

    @pl.loop(0, TALL // 16)
    def _(step):
        row = pl.multiple_of(step * 16, 16)
        near = [distance(x, core, second, row) for second in (False, True)]
        totals = [jnp.zeros((8, 128), jnp.float32)] * NB
        for index, (low, high, e, second) in enumerate(SLABS):
            below, inside = edges_of(low, high)
            v = sums_ref[index + 1, pl.ds(row, 16), :]
            found = [(b, fold(v)) for edge, b in below]
            for edge, b in inside:
                found.append((b, fold(jnp.where(near[second] >= edge - PAIR * e, v, 0.0))))
            for k, (b, total) in enumerate(found):
                totals[b] = totals[b] + total
                if k:
                    totals[found[k - 1][0]] = totals[found[k - 1][0]] - total
        for b in range(NB):
            buckets[b] += totals[b]

    lane = lax.broadcasted_iota(jnp.int32, (8, 128), 1)
    row = jnp.zeros((8, 128), jnp.float32)
    for b in range(NB):
        total = jnp.sum(jnp.sum(buckets[b], axis=0, keepdims=True), axis=1, keepdims=True)
        row = jnp.where(lane == b, total * 0.5, row)
    bias_ref[...] = row


def main_kernel(
    where_ref, bounds_ref, plan_ref, table, own_ref, kvx_ref, kvc_ref, kvxc_ref, qgx_ref,
    keep_ref, give_ref, mine_ref, theirs_ref, biasacc,
    line, kvs, dkv, starts, scales, acc, lhs, qgt, *stages,
):
    x = where_ref[0]
    core = where_ref[1]
    odd = lax.rem(x, 2)
    lower = jnp.minimum(x, 3 - x)

    def aligned(v):
        return pl.multiple_of(v * ROWS, ROWS)

    k_own = aligned(2 * core + odd)
    k_x = aligned(2 * core + 1 - odd)
    k_core = aligned(2 * (1 - core) + odd)
    k_both = aligned(2 * (1 - core) + 1 - odd)
    q_own = aligned((x != lower).astype(jnp.int32))
    q_x = aligned((x == lower).astype(jnp.int32))
    lane = lax.broadcasted_iota(jnp.int32, (TALL, 128), 1)
    left = lane < HD
    row = lax.broadcasted_iota(jnp.int32, (TALL, 128), 0)
    offset = row + jnp.where(row >= ROWS, ROWS * (2 - 2 * lower), 0)

    @pl.loop(0, GROUPS)
    def _(n):
        line[n, pl.ds(k_own, ROWS), :] = own_ref[n, :ROWS]
        line[n, pl.ds(k_x, ROWS), :] = kvx_ref[n]
        line[n, pl.ds(k_core, ROWS), :] = kvc_ref[n]
        line[n, pl.ds(k_both, ROWS), :] = kvxc_ref[n]
        acc[n] = jnp.zeros((TALL, 128), jnp.float32)
        zero = jnp.zeros((ROWS, 128), jnp.bfloat16)
        for at, qg in ((q_own, own_ref[n, ROWS:]), (q_x, qgx_ref[n])):
            lhs[n, pl.ds(at, ROWS), :] = jnp.where(left[:ROWS], qg, zero)
            lhs[n, pl.ds(pl.multiple_of(at + TALL, ROWS), ROWS), :] = jnp.where(left[:ROWS], zero, qg)
        qgt[n] = (lhs[n, pl.ds(0, TALL), :] + lhs[n, pl.ds(TALL, TALL), :]).T
        first, last = span_of(x, core, n)
        pos = first + offset

        def history(d, low):
            begin = bounds_ref[d]
            end = jnp.where(d + 1 < DOCS, bounds_ref[jnp.minimum(d + 1, DOCS - 1)], PAIR * GROUPS)
            inside = pos >= begin
            size = jnp.full((TALL, 128), end - begin, jnp.int32).astype(jnp.float32)
            starts[n] = jnp.where(inside, begin, starts[n])
            scales[n] = jnp.where(left, 0.0625, jnp.where(inside, lax.rsqrt(size), scales[n]))
            return low

        d_first, d_last = jnp.int32(0), jnp.int32(0)
        for d in range(1, DOCS):
            d_first = d_first + (first >= bounds_ref[d]).astype(jnp.int32)
            d_last = d_last + (last >= bounds_ref[d]).astype(jnp.int32)
        starts[n] = jnp.zeros((TALL, 128), jnp.int32)
        scales[n] = jnp.zeros((TALL, 128), jnp.float32)
        lax.fori_loop(d_first, d_last + 1, history, 0)

    @pl.loop(0, GROUPS // 2)
    def _(m):
        kvs[3 * m] = line[2 * m, :WIDE]
        kvs[3 * m + 1] = line[2 * m + 1, :WIDE]
        kvs[3 * m + 2, :128] = line[2 * m, WIDE:]
        kvs[3 * m + 2, 128:] = line[2 * m + 1, WIDE:]
        for r in range(3):
            dkv[3 * m + r] = jnp.zeros((128, WIDE), jnp.float32)

    @pl.loop(0, len(SLABS) + 1)
    def _(e):
        biasacc[e] = jnp.zeros((TALL, WIDE), jnp.float32)

    score, weight = stages[:DEPTH], stages[DEPTH:]
    weight[0][...] = jnp.zeros((2 * TALL, WIDE), jnp.bfloat16)
    j = lax.broadcasted_iota(jnp.int32, (1, WIDE), 1)
    first_lanes, second_lanes = key_lanes(x, j, False), key_lanes(x, j, True)

    def scores(k, s):
        g, n = plan_ref[k], plan_ref[SLOTS + k]
        s[...] = lax.dot_general(lhs[g], kvs[n], NT, preferred_element_type=jnp.float32)

    def weigh(k, s, w_out):
        g, n, e = plan_ref[k], plan_ref[SLOTS + k], plan_ref[2 * SLOTS + k]
        m = lax.div(n, 3)
        key = jnp.where(e > 9, second_lanes, first_lanes)
        key = key + PAIR * (2 * m + (n - 3 * m == 1).astype(jnp.int32))
        begin = jnp.concatenate([starts[g]] * 2, axis=1)
        half = jnp.where(key >= begin, s[pl.ds(0, TALL), :] + table[e], LOW)
        t = jnp.tanh(half)
        u = 1.0 + t
        w = half * u
        ds = s[pl.ds(TALL, TALL), :] * (u + w * (1.0 - t))
        biasacc[e] += ds
        w_out[pl.ds(0, TALL), :] = w.astype(jnp.bfloat16)
        w_out[pl.ds(TALL, TALL), :] = ds.astype(jnp.bfloat16)

    def gather(k, w_in):
        g, n = plan_ref[k], plan_ref[SLOTS + k]
        od = jnp.dot(w_in[...], kvs[n], preferred_element_type=jnp.float32)
        acc[g] += jnp.where(left, od[TALL:], od[:TALL])
        dkv[n, pl.ds(0, HD), :] += jnp.dot(
            qgt[g, pl.ds(0, HD), :], w_in[pl.ds(TALL, TALL), :], preferred_element_type=jnp.float32
        )
        dkv[n, pl.ds(HD, HD), :] += jnp.dot(
            qgt[g, pl.ds(HD, HD), :], w_in[pl.ds(0, TALL), :], preferred_element_type=jnp.float32
        )

    scores(1, score[1])

    @pl.loop(0, lax.div(plan_ref[3 * SLOTS] + DEPTH, DEPTH))
    def _(step):
        for i in range(DEPTH):
            k = DEPTH * step + i
            now, later = (i + 1) % DEPTH, (i + 2) % DEPTH
            gather(k, weight[i])
            weigh(k + 1, score[now], weight[now])
            scores(k + 2, score[later])

    @pl.loop(0, GROUPS // 2)
    def _(m):
        line[2 * m, :WIDE] = dkv[3 * m].astype(jnp.bfloat16).T
        line[2 * m + 1, :WIDE] = dkv[3 * m + 1].astype(jnp.bfloat16).T
        last = dkv[3 * m + 2].astype(jnp.bfloat16).T
        line[2 * m, WIDE:] = last[:128]
        line[2 * m + 1, WIDE:] = last[128:]

    @pl.loop(0, GROUPS)
    def _(n):
        acc[n] = acc[n] * scales[n]
        mine_ref[n] = acc[n, pl.ds(q_own, ROWS), :]
        theirs_ref[n] = acc[n, pl.ds(q_x, ROWS), :].astype(jnp.bfloat16)
        keep_ref[n, :ROWS] = line[n, pl.ds(k_own, ROWS), :]
        keep_ref[n, ROWS:] = line[n, pl.ds(k_x, ROWS), :]
        give_ref[n, :ROWS] = line[n, pl.ds(k_core, ROWS), :]
        give_ref[n, ROWS:] = line[n, pl.ds(k_both, ROWS), :]


def unpack_kernel(in_ref, out_ref, grad_ref):
    for h in range(0, H, 2):
        cols = slice(h * HD, (h + 2) * HD)
        a, b = in_ref[h, :ROWS], in_ref[h + 1, :ROWS]
        grad_ref[0, :, cols] = jnp.concatenate([a[:, :HD], b[:, :HD]], axis=1)
        out_ref[:, cols] = jnp.concatenate([a[:, HD:], b[:, HD:]], axis=1)
        a, b = in_ref[h, ROWS : 2 * ROWS], in_ref[h + 1, ROWS : 2 * ROWS]
        grad_ref[1, :, cols] = jnp.concatenate([a[:, :HD], b[:, :HD]], axis=1)
        grad_ref[2, :, cols] = jnp.concatenate([a[:, HD:], b[:, HD:]], axis=1)


def swap(v, axis, partner):
    return lax.ppermute(v, axis, [(i, p) for i, p in enumerate(partner)])


def per_device(qkv, grad_out, rab, doc_ids):
    bf16, f32 = jnp.bfloat16, jnp.float32
    x, y, z, core = (lax.axis_index(a) for a in ("x", "y", "z", "core"))
    whole = pl.BlockSpec(memory_space=VMEM)
    scalars = pl.BlockSpec(memory_space=SMEM)
    block = jax.ShapeDtypeStruct((H, ROWS, 128), bf16)
    double = jax.ShapeDtypeStruct((H, 2 * ROWS, 128), bf16)
    slabs = jax.ShapeDtypeStruct((len(SLABS) + 1, TALL, WIDE), f32)
    small = pltpu.CompilerParams(vmem_limit_bytes=8 * 2**20)
    large = pltpu.CompilerParams(vmem_limit_bytes=34 * 2**20)
    first_row = (((y * 4 + z) * 2 + core) * 4 + x) * ROWS
    where = jnp.stack([x, core])
    packed, bounds = pl.pallas_call(
        pack_kernel,
        out_shape=(double, jax.ShapeDtypeStruct((DOCS,), jnp.int32)),
        in_specs=[scalars, whole, whole, whole],
        out_specs=(whole, scalars),
        compiler_params=small,
        name="pack",
    )(first_row.reshape(1), doc_ids.reshape(96, 128), qkv.transpose(1, 0, 2), grad_out)
    own = lax.all_to_all(packed, ("y", "z"), 0, 0, tiled=True)
    kv_own, qg_own = own[:, :ROWS], own[:, ROWS:]
    kv_x = swap(kv_own, "x", (1, 0, 3, 2))
    qg_x = swap(qg_own, "x", (3, 2, 1, 0))
    kv_core = swap(kv_own, "core", (1, 0))
    table_row = lax.dynamic_slice_in_dim(rab, y * 4 + z, 1, 0)[0]
    table, plan = pl.pallas_call(
        table_kernel,
        out_shape=(slabs, jax.ShapeDtypeStruct((3 * SLOTS + 1,), jnp.int32)),
        in_specs=[scalars] * 3,
        out_specs=(whole, scalars),
        compiler_params=small,
        cost_estimate=pl.CostEstimate(flops=0, bytes_accessed=0, transcendentals=0),
        name="table",
    )(where, table_row, bounds)
    kv_x, qg_x, table, plan = lax.optimization_barrier((kv_x, qg_x, table, plan))
    kv_both = swap(kv_x, "core", (1, 0))
    keep, give, mine, theirs, sums = pl.pallas_call(
        main_kernel,
        out_shape=[double, double, jax.ShapeDtypeStruct((H, ROWS, 128), f32), block, slabs],
        in_specs=[scalars] * 3 + [whole] * 6,
        out_specs=[whole] * 5,
        scratch_shapes=[
            VMEM((GROUPS, SUPER, 128), bf16),
            VMEM((24, WIDE, 128), bf16),
            VMEM((24, 128, WIDE), f32),
            VMEM((GROUPS, TALL, 128), jnp.int32),
            VMEM((GROUPS, TALL, 128), f32),
            VMEM((GROUPS, TALL, 128), f32),
            VMEM((GROUPS, 2 * TALL, 128), bf16),
            VMEM((GROUPS, 128, TALL), bf16),
        ]
        + [VMEM((2 * TALL, WIDE), f32)] * DEPTH
        + [VMEM((2 * TALL, WIDE), bf16)] * DEPTH,
        compiler_params=large,
        name="attend",
    )(where, bounds, plan, table, own, kv_x, kv_core, kv_both, qg_x)
    got = swap(give, "core", (1, 0))
    dkv = keep.astype(f32) + got.astype(f32)
    dkv_x = dkv[:, ROWS:].astype(bf16)
    got_qo = swap(theirs, "x", (3, 2, 1, 0))
    got_dkv = swap(dkv_x, "x", (1, 0, 3, 2))
    bias = pl.pallas_call(
        buckets_kernel,
        out_shape=jax.ShapeDtypeStruct((8, 128), f32),
        in_specs=[scalars, whole],
        out_specs=whole,
        scratch_shapes=[VMEM((NB, 8, 128), f32)],
        compiler_params=small,
        cost_estimate=pl.CostEstimate(flops=0, bytes_accessed=0, transcendentals=0),
        name="buckets",
    )(where, sums)
    bias = bias + sum(swap(bias, "x", p) for p in ((1, 0, 3, 2), (3, 2, 1, 0), (2, 3, 0, 1)))
    bias = bias[0]
    hi = lax.reduce_precision(bias, 8, 7)
    mid = lax.reduce_precision(bias - hi, 8, 7)
    lo = bias - hi - mid
    carried = jnp.pad(jnp.stack([hi, mid, lo]).astype(bf16), ((0, 13), (0, 0)))
    results = jnp.concatenate(
        [
            (mine + got_qo.astype(f32)).astype(bf16),
            (dkv[:, :ROWS] + got_dkv.astype(f32)).astype(bf16),
            jnp.broadcast_to(carried[None], (H, 16, 128)),
        ],
        axis=1,
    )
    results = lax.all_to_all(results, ("y", "z"), 0, 0, tiled=True)
    terms = lax.dynamic_slice(results, (x * 4, 2 * ROWS, 0), (4, 3, NB)).astype(f32)
    bias_grad = terms[:, 0] + terms[:, 1] + terms[:, 2]
    bias_grad = bias_grad + swap(bias_grad, "core", (1, 0))
    out, grad_qkv = pl.pallas_call(
        unpack_kernel,
        out_shape=(
            jax.ShapeDtypeStruct((ROWS, H * HD), bf16),
            jax.ShapeDtypeStruct((3, ROWS, H * HD), bf16),
        ),
        in_specs=[whole],
        out_specs=(whole, whole),
        compiler_params=small,
        name="unpack",
    )(results)
    return out, grad_qkv.transpose(1, 0, 2), bias_grad


def solution(mesh):
    fine = Mesh(mesh.devices.reshape(4, 4, 4, 2), ("x", "y", "z", "core"))
    rows = ("y", "z", "core", "x")
    return jax.shard_map(
        per_device,
        mesh=fine,
        in_specs=(P(rows, None, None), P(rows, None), P(), P()),
        out_specs=(P(rows, None), P(rows, None, None), P("x", None)),
        check_vma=False,
    )
```

```python
import jax
import jax.numpy as jnp
from jax import lax
from jax.experimental import pallas as pl
from jax.experimental.pallas import tpu as pltpu
from jax.sharding import Mesh
from jax.sharding import PartitionSpec as P

HD = 64
H = 16
NB = 20
DOCS = 8
ROWS = 96
SUPER = 384
GROUPS = 16
PAIR = 768
TALL = 192
WIDE = 256
CHUNK = 128
SLOTS = 256
DEPTH = 6
LOW = -1e30
VMEM = pltpu.VMEM
SMEM = pltpu.SMEM
NT = (((1,), (1,)), ((), ()))


def doc_bounds(ids):
    return [jnp.int32(0)] + [
        jnp.sum((ids < d).astype(jnp.float32)).astype(jnp.int32) for d in range(1, DOCS)
    ]


def pack_kernel(where_ref, ids, qkv, g_in, out_ref, bounds_ref, ids_ref, qkv_ref, g_ref, sems):
    copies = [
        pltpu.make_async_copy(source, target, sems.at[k])
        for k, (source, target) in enumerate(((ids, ids_ref), (qkv, qkv_ref), (g_in, g_ref)))
    ]
    for copy in copies:
        copy.start()
    copies[0].wait()
    bounds = doc_bounds(ids_ref[...])
    for d in range(DOCS):
        bounds_ref[d] = bounds[d]
    pos = where_ref[0] + lax.broadcasted_iota(jnp.int32, (ROWS, 128), 0)
    length = jnp.zeros((ROWS, 128), jnp.int32)
    ends = bounds[1:] + [jnp.int32(PAIR * GROUPS)]
    for d in range(DOCS):
        length = jnp.where(pos >= bounds[d], ends[d] - bounds[d], length)
    scale = lax.rsqrt(length.astype(jnp.float32))[:, :HD]
    copies[1].wait()
    copies[2].wait()
    for h in range(H):
        cols = slice(h * HD, (h + 1) * HD)
        out_ref[h, :ROWS] = jnp.concatenate([qkv_ref[1, :, cols], qkv_ref[2, :, cols]], axis=1)
        q = (qkv_ref[0, :, cols].astype(jnp.float32) * 0.0625).astype(jnp.bfloat16)
        g = (g_ref[:, cols].astype(jnp.float32) * scale).astype(jnp.bfloat16)
        out_ref[h, ROWS:] = jnp.concatenate([q, g], axis=1)


EDGES = [(k, k) for k in range(8)] + [(2**p, p + 6) for p in range(3, 13)]


def edges_of(low, high):
    below = [edge for edge in EDGES if edge[0] <= low]
    return below[-1:], [edge for edge in EDGES if low < edge[0] <= high]


def key_place(x, c, lane):
    j = CHUNK * c + lane
    return j + 2 * ROWS * lax.div(x, 2) + jnp.where(j >= 2 * ROWS, SUPER - 2 * ROWS, 0)


SLABS = [
    (c, e, PAIR * e - (319, 639, 767)[c], PAIR * e + PAIR - 1 - (0, 128, 448)[c])
    for c in range(3)
    for e in range(9)
]


def distance(x, core, c, row):
    i = row + lax.broadcasted_iota(jnp.int32, (16, CHUNK), 0)
    lane = lax.broadcasted_iota(jnp.int32, (16, CHUNK), 1)
    lower = jnp.minimum(x, 3 - x)
    i = i + ROWS * lower + jnp.where(i >= ROWS, ROWS * (2 - 2 * lower), 0)
    return SUPER * core + i - key_place(x, c, lane)


def start_of(bounds_ref, pos):
    start = jnp.int32(0)
    for d in range(1, DOCS):
        start = jnp.where(pos >= bounds_ref[d], bounds_ref[d], start)
    return start


def span_of(x, core, g):
    lower = jnp.minimum(x, 3 - x)
    base = PAIR * g + SUPER * core
    return base + ROWS * lower, base + ROWS * (4 - lower) - 1


def table_kernel(where_ref, rab_ref, bounds_ref, table_ref, starts_ref, scales_ref, plan_ref):
    x, core = where_ref[0], where_ref[1]
    column = 2 * ROWS * lax.div(x, 2)

    def of_group(g, at):
        first, last = span_of(x, core, g)
        begin = start_of(bounds_ref, first)

        def of_pair(n, at):
            for c, (low, high) in enumerate(((0, 127), (128, 447), (448, 575))):
                place = PAIR * n + column
                live = (place + high >= begin) & (place + low <= last)
                plan_ref[lax.div(at, 2)] = g
                plan_ref[SLOTS + at] = 3 * n + c
                plan_ref[3 * SLOTS + at] = 9 * c + g - n + 1
                at = at + live.astype(jnp.int32)
            return at

        at = lax.fori_loop(lax.div(begin, PAIR), g + 1, of_pair, at)
        plan_ref[SLOTS + at] = 0
        plan_ref[3 * SLOTS + at] = 0
        return at + lax.rem(at, 2)

    at = lax.fori_loop(0, GROUPS, of_group, jnp.int32(2))
    tiles = lax.div(at, 2)
    plan_ref[5 * SLOTS] = tiles - 1
    plan_ref[0] = 0
    for extra in range(DEPTH + 1):
        plan_ref[tiles + extra] = 0
    for half in range(2):
        plan_ref[SLOTS + half] = 0
        plan_ref[3 * SLOTS + half] = 0
        for extra in range(DEPTH + 1):
            plan_ref[SLOTS + at + 2 * extra + half] = 0
            plan_ref[3 * SLOTS + at + 2 * extra + half] = 0

    table_ref[0] = jnp.full((TALL, CHUNK), LOW, jnp.float32)

    @pl.loop(0, TALL // 16)
    def _(step):
        row = pl.multiple_of(step * 16, 16)
        near = [distance(x, core, c, row) for c in range(3)]
        for index, (c, e, low, high) in enumerate(SLABS):
            below, inside = edges_of(low, high)
            value = jnp.full((16, CHUNK), rab_ref[below[0][1]] * 0.5 if below else LOW, jnp.float32)
            for edge, b in inside:
                value = jnp.where(near[c] >= edge - PAIR * e, rab_ref[b] * 0.5, value)
            table_ref[index + 1, pl.ds(row, 16), :] = value

    left = lax.broadcasted_iota(jnp.int32, (TALL, 128), 1) < HD
    row = lax.broadcasted_iota(jnp.int32, (TALL, 128), 0)
    offset = row + jnp.where(row >= ROWS, ROWS * (2 - 2 * jnp.minimum(x, 3 - x)), 0)

    @pl.loop(0, GROUPS)
    def _(g):
        first, last = span_of(x, core, g)
        pos = first + offset
        d_first, d_last = jnp.int32(0), jnp.int32(0)
        for d in range(1, DOCS):
            d_first = d_first + (first >= bounds_ref[d]).astype(jnp.int32)
            d_last = d_last + (last >= bounds_ref[d]).astype(jnp.int32)
        starts_ref[g] = jnp.zeros((TALL, 128), jnp.int32)
        scales_ref[g] = jnp.zeros((TALL, 128), jnp.float32)

        def history(d, carry):
            begin = bounds_ref[d]
            end = jnp.where(d + 1 < DOCS, bounds_ref[jnp.minimum(d + 1, DOCS - 1)], PAIR * GROUPS)
            inside = pos >= begin
            size = jnp.full((TALL, 128), end - begin, jnp.int32).astype(jnp.float32)
            starts_ref[g] = jnp.where(inside, begin, starts_ref[g])
            scales_ref[g] = jnp.where(
                left, 0.0625, jnp.where(inside, lax.rsqrt(size), scales_ref[g])
            )
            return carry

        lax.fori_loop(d_first, d_last + 1, history, 0)


def buckets_kernel(where_ref, sums_ref, bias_ref, buckets):
    x, core = where_ref[0], where_ref[1]
    buckets[...] = jnp.zeros((NB, 8, 128), jnp.float32)

    @pl.loop(0, TALL // 16)
    def _(step):
        row = pl.multiple_of(step * 16, 16)
        near = [distance(x, core, c, row) for c in range(3)]
        totals = [jnp.zeros((8, 128), jnp.float32)] * NB
        for index, (c, e, low, high) in enumerate(SLABS):
            below, inside = edges_of(low, high)
            v = sums_ref[index + 1, pl.ds(row, 16), :]
            found = [(b, v[:8] + v[8:]) for edge, b in below]
            for edge, b in inside:
                part = jnp.where(near[c] >= edge - PAIR * e, v, 0.0)
                found.append((b, part[:8] + part[8:]))
            for k, (b, total) in enumerate(found):
                totals[b] = totals[b] + total
                if k:
                    totals[found[k - 1][0]] = totals[found[k - 1][0]] - total
        for b in range(NB):
            buckets[b] += totals[b]

    lane = lax.broadcasted_iota(jnp.int32, (8, 128), 1)
    row = jnp.zeros((8, 128), jnp.float32)
    for b in range(NB):
        total = jnp.sum(jnp.sum(buckets[b], axis=0, keepdims=True), axis=1, keepdims=True)
        row = jnp.where(lane == b, total * 0.5, row)
    bias_ref[...] = row


def main_kernel(
    where_ref, plan_ref, table, starts, scales, own_ref, kvx_ref, kvc_ref, kvxc_ref, qgx_ref,
    keep_ref, give_ref, mine_ref, theirs_ref, biasacc,
    line, dkv, acc, lhs, qgt, *stages,
):
    x = where_ref[0]
    core = where_ref[1]
    odd = lax.rem(x, 2)
    lower = jnp.minimum(x, 3 - x)

    def aligned(v):
        return pl.multiple_of(v * ROWS, ROWS)

    k_own = aligned(2 * core + odd)
    k_x = aligned(2 * core + 1 - odd)
    k_core = aligned(2 * (1 - core) + odd)
    k_both = aligned(2 * (1 - core) + 1 - odd)
    q_own = aligned((x != lower).astype(jnp.int32))
    q_x = aligned((x == lower).astype(jnp.int32))
    lane = lax.broadcasted_iota(jnp.int32, (TALL, 128), 1)
    left = lane < HD

    def chunk(k):
        return pl.ds(pl.multiple_of(CHUNK * k, CHUNK), CHUNK)

    def block(n, at):
        return pl.ds(pl.multiple_of(SUPER * n + at, ROWS), ROWS)

    @pl.loop(0, GROUPS)
    def _(n):
        line[block(n, k_own), :] = own_ref[n, :ROWS]
        line[block(n, k_x), :] = kvx_ref[n]
        line[block(n, k_core), :] = kvc_ref[n]
        line[block(n, k_both), :] = kvxc_ref[n]
        for c in range(3):
            dkv[3 * n + c] = jnp.zeros((128, CHUNK), jnp.float32)
        acc[n] = jnp.zeros((TALL, 128), jnp.float32)
        zero = jnp.zeros((ROWS, 128), jnp.bfloat16)
        for at, qg in ((q_own, own_ref[n, ROWS:]), (q_x, qgx_ref[n])):
            lhs[n, pl.ds(at, ROWS), :] = jnp.where(left[:ROWS], qg, zero)
            lhs[n, pl.ds(pl.multiple_of(at + TALL, ROWS), ROWS), :] = jnp.where(left[:ROWS], zero, qg)
        qgt[n] = (lhs[n, pl.ds(0, TALL), :] + lhs[n, pl.ds(TALL, TALL), :]).T

    @pl.loop(0, len(SLABS) + 1)
    def _(e):
        biasacc[e] = jnp.zeros((TALL, CHUNK), jnp.float32)

    score, weight = stages[:DEPTH], stages[DEPTH:]
    weight[0][...] = jnp.zeros((2 * TALL, WIDE), jnp.bfloat16)
    lanes = lax.broadcasted_iota(jnp.int32, (1, CHUNK), 1)
    places = [key_place(x, c, lanes) for c in range(3)]
    halves = (slice(0, CHUNK), slice(CHUNK, WIDE))

    def entry(k):
        chunks = [plan_ref[SLOTS + 2 * k + half] for half in range(2)]
        slabs = [plan_ref[3 * SLOTS + 2 * k + half] for half in range(2)]
        return plan_ref[k], chunks, slabs

    def scores(k, s):
        g, chunks, slabs = entry(k)
        for cols, n in zip(halves, chunks):
            s[:, cols] = lax.dot_general(
                lhs[g], line[chunk(n), :], NT, preferred_element_type=jnp.float32
            )

    def weigh(k, s, w_out):
        g, chunks, slabs = entry(k)
        for cols, n, e in zip(halves, chunks, slabs):
            pair = lax.div(n, 3)
            c = n - 3 * pair
            key = PAIR * pair + jnp.where(c == 0, places[0], jnp.where(c == 1, places[1], places[2]))
            half = s[pl.ds(0, TALL), cols] + table[e]
            half = jnp.where(key >= starts[g], half, LOW)
            t = jnp.tanh(half)
            u = 1.0 + t
            w = half * u
            ds = s[pl.ds(TALL, TALL), cols] * (u + w * (1.0 - t))
            biasacc[e] += ds
            w_out[pl.ds(0, TALL), cols] = w.astype(jnp.bfloat16)
            w_out[pl.ds(TALL, TALL), cols] = ds.astype(jnp.bfloat16)

    def gather(k, w_in):
        g, chunks, slabs = entry(k)
        keyvals = jnp.concatenate([line[chunk(n), :] for n in chunks], axis=0)
        od = jnp.dot(w_in[...], keyvals, preferred_element_type=jnp.float32)
        acc[g] += jnp.where(left, od[TALL:], od[:TALL])
        for rows, low in ((pl.ds(0, HD), TALL), (pl.ds(HD, HD), 0)):
            part = jnp.dot(
                qgt[g, rows, :], w_in[pl.ds(low, TALL), :], preferred_element_type=jnp.float32
            )
            for cols, n in zip(halves, chunks):
                dkv[n, rows, :] += part[:, cols]

    scores(1, score[1])

    @pl.loop(0, lax.div(plan_ref[5 * SLOTS] + DEPTH, DEPTH))
    def _(step):
        for i in range(DEPTH):
            k = DEPTH * step + i
            now, later = (i + 1) % DEPTH, (i + 2) % DEPTH
            gather(k, weight[i])
            weigh(k + 1, score[now], weight[now])
            scores(k + 2, score[later])

    @pl.loop(0, GROUPS)
    def _(n):
        for c in range(3):
            line[chunk(3 * n + c), :] = dkv[3 * n + c].astype(jnp.bfloat16).T
        acc[n] = acc[n] * scales[n]
        mine_ref[n] = acc[n, pl.ds(q_own, ROWS), :]
        theirs_ref[n] = acc[n, pl.ds(q_x, ROWS), :].astype(jnp.bfloat16)
        keep_ref[n, :ROWS] = line[block(n, k_own), :]
        keep_ref[n, ROWS:] = line[block(n, k_x), :]
        give_ref[n, :ROWS] = line[block(n, k_core), :]
        give_ref[n, ROWS:] = line[block(n, k_both), :]


def unpack_kernel(in_ref, out_ref, grad_ref):
    for h in range(0, H, 2):
        cols = slice(h * HD, (h + 2) * HD)
        a, b = in_ref[h, :ROWS], in_ref[h + 1, :ROWS]
        grad_ref[0, :, cols] = jnp.concatenate([a[:, :HD], b[:, :HD]], axis=1)
        out_ref[:, cols] = jnp.concatenate([a[:, HD:], b[:, HD:]], axis=1)
        a, b = in_ref[h, ROWS : 2 * ROWS], in_ref[h + 1, ROWS : 2 * ROWS]
        grad_ref[1, :, cols] = jnp.concatenate([a[:, :HD], b[:, :HD]], axis=1)
        grad_ref[2, :, cols] = jnp.concatenate([a[:, HD:], b[:, HD:]], axis=1)


def swap(v, axis, partner):
    return lax.ppermute(v, axis, [(i, p) for i, p in enumerate(partner)])


def per_device(qkv, grad_out, rab, doc_ids):
    bf16, f32 = jnp.bfloat16, jnp.float32
    x, y, z, core = (lax.axis_index(a) for a in ("x", "y", "z", "core"))
    whole = pl.BlockSpec(memory_space=VMEM)
    scalars = pl.BlockSpec(memory_space=SMEM)
    block = jax.ShapeDtypeStruct((H, ROWS, 128), bf16)
    double = jax.ShapeDtypeStruct((H, 2 * ROWS, 128), bf16)
    slabs = jax.ShapeDtypeStruct((len(SLABS) + 1, TALL, CHUNK), f32)
    small = pltpu.CompilerParams(vmem_limit_bytes=8 * 2**20)
    large = pltpu.CompilerParams(vmem_limit_bytes=34 * 2**20)
    first_row = (((y * 4 + z) * 2 + core) * 4 + x) * ROWS
    where = jnp.stack([x, core])
    packed, bounds = pl.pallas_call(
        pack_kernel,
        out_shape=(double, jax.ShapeDtypeStruct((DOCS,), jnp.int32)),
        in_specs=[scalars] + [pl.BlockSpec(memory_space=pltpu.HBM)] * 3,
        out_specs=(whole, scalars),
        scratch_shapes=[
            VMEM((96, 128), jnp.int32),
            VMEM((3, ROWS, H * HD), bf16),
            VMEM((ROWS, H * HD), bf16),
            pltpu.SemaphoreType.DMA((3,)),
        ],
        compiler_params=pltpu.CompilerParams(vmem_limit_bytes=63 * 2**20),
        name="pack",
    )(first_row.reshape(1), doc_ids.reshape(96, 128), qkv.transpose(1, 0, 2), grad_out)
    own = lax.all_to_all(packed, ("y", "z"), 0, 0, tiled=True)
    kv_own, qg_own = own[:, :ROWS], own[:, ROWS:]
    kv_x = swap(kv_own, "x", (1, 0, 3, 2))
    qg_x = swap(qg_own, "x", (3, 2, 1, 0))
    kv_core = swap(kv_own, "core", (1, 0))
    table_row = lax.dynamic_slice_in_dim(rab, y * 4 + z, 1, 0)[0]
    table, starts, scales, plan = pl.pallas_call(
        table_kernel,
        out_shape=(
            slabs,
            jax.ShapeDtypeStruct((GROUPS, TALL, 128), jnp.int32),
            jax.ShapeDtypeStruct((GROUPS, TALL, 128), f32),
            jax.ShapeDtypeStruct((5 * SLOTS + 1,), jnp.int32),
        ),
        in_specs=[scalars] * 3,
        out_specs=(whole, whole, whole, scalars),
        compiler_params=small,
        cost_estimate=pl.CostEstimate(flops=0, bytes_accessed=0, transcendentals=0),
        name="table",
    )(where, table_row, bounds)
    kv_x, qg_x, table, starts, scales, plan = lax.optimization_barrier(
        (kv_x, qg_x, table, starts, scales, plan)
    )
    kv_both = swap(kv_x, "core", (1, 0))
    keep, give, mine, theirs, sums = pl.pallas_call(
        main_kernel,
        out_shape=[double, double, jax.ShapeDtypeStruct((H, ROWS, 128), f32), block, slabs],
        in_specs=[scalars] * 2 + [whole] * 8,
        out_specs=[whole] * 5,
        scratch_shapes=[
            VMEM((GROUPS * SUPER, 128), bf16),
            VMEM((3 * GROUPS, 128, CHUNK), f32),
            VMEM((GROUPS, TALL, 128), f32),
            VMEM((GROUPS, 2 * TALL, 128), bf16),
            VMEM((GROUPS, 128, TALL), bf16),
        ]
        + [VMEM((2 * TALL, WIDE), f32)] * DEPTH
        + [VMEM((2 * TALL, WIDE), bf16)] * DEPTH,
        compiler_params=large,
        name="attend",
    )(where, plan, table, starts, scales, own, kv_x, kv_core, kv_both, qg_x)
    got = swap(give, "core", (1, 0))
    dkv = keep.astype(f32) + got.astype(f32)
    dkv_x = dkv[:, ROWS:].astype(bf16)
    got_qo = swap(theirs, "x", (3, 2, 1, 0))
    got_dkv = swap(dkv_x, "x", (1, 0, 3, 2))
    bias = pl.pallas_call(
        buckets_kernel,
        out_shape=jax.ShapeDtypeStruct((8, 128), f32),
        in_specs=[scalars, whole],
        out_specs=whole,
        scratch_shapes=[VMEM((NB, 8, 128), f32)],
        compiler_params=small,
        cost_estimate=pl.CostEstimate(flops=0, bytes_accessed=0, transcendentals=0),
        name="buckets",
    )(where, sums)
    bias = bias + sum(swap(bias, "x", p) for p in ((1, 0, 3, 2), (3, 2, 1, 0), (2, 3, 0, 1)))
    bias = bias[0]
    hi = lax.reduce_precision(bias, 8, 7)
    mid = lax.reduce_precision(bias - hi, 8, 7)
    lo = bias - hi - mid
    carried = jnp.pad(jnp.stack([hi, mid, lo]).astype(bf16), ((0, 13), (0, 0)))
    results = jnp.concatenate(
        [
            (mine + got_qo.astype(f32)).astype(bf16),
            (dkv[:, :ROWS] + got_dkv.astype(f32)).astype(bf16),
            jnp.broadcast_to(carried[None], (H, 16, 128)),
        ],
        axis=1,
    )
    results = lax.all_to_all(results, ("y", "z"), 0, 0, tiled=True)
    terms = lax.dynamic_slice(results, (x * 4, 2 * ROWS, 0), (4, 3, NB)).astype(f32)
    bias_grad = terms[:, 0] + terms[:, 1] + terms[:, 2]
    bias_grad = bias_grad + swap(bias_grad, "core", (1, 0))
    out, grad_qkv = pl.pallas_call(
        unpack_kernel,
        out_shape=(
            jax.ShapeDtypeStruct((ROWS, H * HD), bf16),
            jax.ShapeDtypeStruct((3, ROWS, H * HD), bf16),
        ),
        in_specs=[whole],
        out_specs=(whole, whole),
        compiler_params=small,
        name="unpack",
    )(results)
    return out, grad_qkv.transpose(1, 0, 2), bias_grad


def solution(mesh):
    fine = Mesh(mesh.devices.reshape(4, 4, 4, 2), ("x", "y", "z", "core"))
    rows = ("y", "z", "core", "x")
    return jax.shard_map(
        per_device,
        mesh=fine,
        in_specs=(P(rows, None, None), P(rows, None), P(), P()),
        out_specs=(P(rows, None), P(rows, None, None), P("x", None)),
        check_vma=False,
    )
```

```python
import jax
import jax.numpy as jnp
from jax import lax
from jax.experimental import pallas as pl
from jax.experimental.pallas import tpu as pltpu
from jax.sharding import Mesh
from jax.sharding import PartitionSpec as P

HD = 64
H = 16
NB = 20
DOCS = 8
ROWS = 96
SUPER = 384
GROUPS = 16
PAIR = 768
TALL = 192
WIDE = 256
CHUNK = 128
SLOTS = 256
DEPTH = 6
LOW = -1e30
VMEM = pltpu.VMEM
SMEM = pltpu.SMEM
NT = (((1,), (1,)), ((), ()))


def doc_bounds(ids):
    return [jnp.int32(0)] + [
        jnp.sum((ids < d).astype(jnp.float32)).astype(jnp.int32) for d in range(1, DOCS)
    ]


def pack_kernel(where_ref, ids, qkv, g_in, out_ref, bounds_ref, ids_ref, qkv_ref, g_ref, sems):
    copies = [
        pltpu.make_async_copy(source, target, sems.at[k])
        for k, (source, target) in enumerate(((ids, ids_ref), (qkv, qkv_ref), (g_in, g_ref)))
    ]
    for copy in copies:
        copy.start()
    copies[0].wait()
    bounds = doc_bounds(ids_ref[...])
    for d in range(DOCS):
        bounds_ref[d] = bounds[d]
    pos = where_ref[0] + lax.broadcasted_iota(jnp.int32, (ROWS, 128), 0)
    length = jnp.zeros((ROWS, 128), jnp.int32)
    ends = bounds[1:] + [jnp.int32(PAIR * GROUPS)]
    for d in range(DOCS):
        length = jnp.where(pos >= bounds[d], ends[d] - bounds[d], length)
    scale = lax.rsqrt(length.astype(jnp.float32))[:, :HD]
    copies[1].wait()
    copies[2].wait()
    for h in range(H):
        cols = slice(h * HD, (h + 1) * HD)
        out_ref[h, :ROWS] = jnp.concatenate([qkv_ref[1, :, cols], qkv_ref[2, :, cols]], axis=1)
        q = (qkv_ref[0, :, cols].astype(jnp.float32) * 0.0625).astype(jnp.bfloat16)
        g = (g_ref[:, cols].astype(jnp.float32) * scale).astype(jnp.bfloat16)
        out_ref[h, ROWS:] = jnp.concatenate([q, g], axis=1)


EDGES = [(k, k) for k in range(8)] + [(2**p, p + 6) for p in range(3, 13)]


def edges_of(low, high):
    below = [edge for edge in EDGES if edge[0] <= low]
    return below[-1:], [edge for edge in EDGES if low < edge[0] <= high]


def key_place(x, c, lane):
    j = CHUNK * c + lane
    return j + 2 * ROWS * lax.div(x, 2) + jnp.where(j >= 2 * ROWS, SUPER - 2 * ROWS, 0)


SLABS = [
    (c, e, PAIR * e - (319, 639, 767)[c], PAIR * e + PAIR - 1 - (0, 128, 448)[c])
    for c in range(3)
    for e in range(9)
]


def distance(x, core, c, row):
    i = row + lax.broadcasted_iota(jnp.int32, (16, CHUNK), 0)
    lane = lax.broadcasted_iota(jnp.int32, (16, CHUNK), 1)
    lower = jnp.minimum(x, 3 - x)
    i = i + ROWS * lower + jnp.where(i >= ROWS, ROWS * (2 - 2 * lower), 0)
    return SUPER * core + i - key_place(x, c, lane)


def start_of(bounds_ref, pos):
    start = jnp.int32(0)
    for d in range(1, DOCS):
        start = jnp.where(pos >= bounds_ref[d], bounds_ref[d], start)
    return start


def span_of(x, core, g):
    lower = jnp.minimum(x, 3 - x)
    base = PAIR * g + SUPER * core
    return base + ROWS * lower, base + ROWS * (4 - lower) - 1


def table_kernel(where_ref, rab_ref, bounds_ref, table_ref, starts_ref, scales_ref, plan_ref):
    x, core = where_ref[0], where_ref[1]
    column = 2 * ROWS * lax.div(x, 2)

    def of_group(g, at):
        first, last = span_of(x, core, g)
        begin = start_of(bounds_ref, first)

        def of_pair(n, at):
            for c, (low, high) in enumerate(((0, 127), (128, 447), (448, 575))):
                place = PAIR * n + column
                live = (place + high >= begin) & (place + low <= last)
                plan_ref[lax.div(at, 2)] = g
                plan_ref[SLOTS + at] = 3 * n + c
                plan_ref[3 * SLOTS + at] = 9 * c + g - n + 1
                at = at + live.astype(jnp.int32)
            return at

        at = lax.fori_loop(lax.div(begin, PAIR), g + 1, of_pair, at)
        plan_ref[SLOTS + at] = 0
        plan_ref[3 * SLOTS + at] = 0
        return at + lax.rem(at, 2)

    at = lax.fori_loop(0, GROUPS, of_group, jnp.int32(2))
    tiles = lax.div(at, 2)
    plan_ref[5 * SLOTS] = tiles - 1
    plan_ref[0] = 0
    for extra in range(DEPTH + 1):
        plan_ref[tiles + extra] = 0
    for half in range(2):
        plan_ref[SLOTS + half] = 0
        plan_ref[3 * SLOTS + half] = 0
        for extra in range(DEPTH + 1):
            plan_ref[SLOTS + at + 2 * extra + half] = 0
            plan_ref[3 * SLOTS + at + 2 * extra + half] = 0

    table_ref[0] = jnp.full((TALL, CHUNK), LOW, jnp.float32)

    @pl.loop(0, TALL // 16)
    def _(step):
        row = pl.multiple_of(step * 16, 16)
        near = [distance(x, core, c, row) for c in range(3)]
        for index, (c, e, low, high) in enumerate(SLABS):
            below, inside = edges_of(low, high)
            value = jnp.full((16, CHUNK), rab_ref[below[0][1]] * 0.5 if below else LOW, jnp.float32)
            for edge, b in inside:
                value = jnp.where(near[c] >= edge - PAIR * e, rab_ref[b] * 0.5, value)
            table_ref[index + 1, pl.ds(row, 16), :] = value

    left = lax.broadcasted_iota(jnp.int32, (TALL, 128), 1) < HD
    row = lax.broadcasted_iota(jnp.int32, (TALL, 128), 0)
    offset = row + jnp.where(row >= ROWS, ROWS * (2 - 2 * jnp.minimum(x, 3 - x)), 0)

    @pl.loop(0, GROUPS)
    def _(g):
        first, last = span_of(x, core, g)
        pos = first + offset
        d_first, d_last = jnp.int32(0), jnp.int32(0)
        for d in range(1, DOCS):
            d_first = d_first + (first >= bounds_ref[d]).astype(jnp.int32)
            d_last = d_last + (last >= bounds_ref[d]).astype(jnp.int32)
        starts_ref[g] = jnp.zeros((TALL, 128), jnp.int32)
        scales_ref[g] = jnp.zeros((TALL, 128), jnp.float32)

        def history(d, carry):
            begin = bounds_ref[d]
            end = jnp.where(d + 1 < DOCS, bounds_ref[jnp.minimum(d + 1, DOCS - 1)], PAIR * GROUPS)
            inside = pos >= begin
            size = jnp.full((TALL, 128), end - begin, jnp.int32).astype(jnp.float32)
            starts_ref[g] = jnp.where(inside, begin, starts_ref[g])
            scales_ref[g] = jnp.where(
                left, 0.0625, jnp.where(inside, lax.rsqrt(size), scales_ref[g])
            )
            return carry

        lax.fori_loop(d_first, d_last + 1, history, 0)


def buckets_kernel(where_ref, sums_ref, bias_ref, buckets):
    x, core = where_ref[0], where_ref[1]
    buckets[...] = jnp.zeros((NB, 8, 128), jnp.float32)

    @pl.loop(0, TALL // 16)
    def _(step):
        row = pl.multiple_of(step * 16, 16)
        near = [distance(x, core, c, row) for c in range(3)]
        totals = [jnp.zeros((8, 128), jnp.float32)] * NB
        for index, (c, e, low, high) in enumerate(SLABS):
            below, inside = edges_of(low, high)
            v = sums_ref[index + 1, pl.ds(row, 16), :]
            found = [(b, v[:8] + v[8:]) for edge, b in below]
            for edge, b in inside:
                part = jnp.where(near[c] >= edge - PAIR * e, v, 0.0)
                found.append((b, part[:8] + part[8:]))
            for k, (b, total) in enumerate(found):
                totals[b] = totals[b] + total
                if k:
                    totals[found[k - 1][0]] = totals[found[k - 1][0]] - total
        for b in range(NB):
            buckets[b] += totals[b]

    lane = lax.broadcasted_iota(jnp.int32, (8, 128), 1)
    row = jnp.zeros((8, 128), jnp.float32)
    for b in range(NB):
        total = jnp.sum(jnp.sum(buckets[b], axis=0, keepdims=True), axis=1, keepdims=True)
        row = jnp.where(lane == b, total * 0.5, row)
    bias_ref[...] = row


def main_kernel(
    where_ref, plan_ref, table, starts, scales, own_ref, kvx_ref, kvc_ref, kvxc_ref, qgx_ref,
    keep_ref, give_ref, mine_ref, theirs_ref, biasacc,
    line, dkv, acc, lhs, qgt, *stages,
):
    x = where_ref[0]
    core = where_ref[1]
    odd = lax.rem(x, 2)
    lower = jnp.minimum(x, 3 - x)

    def aligned(v):
        return pl.multiple_of(v * ROWS, ROWS)

    k_own = aligned(2 * core + odd)
    k_x = aligned(2 * core + 1 - odd)
    k_core = aligned(2 * (1 - core) + odd)
    k_both = aligned(2 * (1 - core) + 1 - odd)
    q_own = aligned((x != lower).astype(jnp.int32))
    q_x = aligned((x == lower).astype(jnp.int32))
    lane = lax.broadcasted_iota(jnp.int32, (TALL, 128), 1)
    left = lane < HD

    def chunk(k):
        return pl.ds(pl.multiple_of(CHUNK * k, CHUNK), CHUNK)

    def block(n, at):
        return pl.ds(pl.multiple_of(SUPER * n + at, ROWS), ROWS)

    @pl.loop(0, GROUPS)
    def _(n):
        line[block(n, k_own), :] = own_ref[n, :ROWS]
        line[block(n, k_x), :] = kvx_ref[n]
        line[block(n, k_core), :] = kvc_ref[n]
        line[block(n, k_both), :] = kvxc_ref[n]
        for c in range(3):
            dkv[3 * n + c] = jnp.zeros((128, CHUNK), jnp.float32)
        acc[n] = jnp.zeros((TALL, 128), jnp.float32)
        zero = jnp.zeros((ROWS, 128), jnp.bfloat16)
        for at, qg in ((q_own, own_ref[n, ROWS:]), (q_x, qgx_ref[n])):
            lhs[n, pl.ds(at, ROWS), :] = jnp.where(left[:ROWS], qg, zero)
            lhs[n, pl.ds(pl.multiple_of(at + TALL, ROWS), ROWS), :] = jnp.where(left[:ROWS], zero, qg)
        qgt[n] = (lhs[n, pl.ds(0, TALL), :] + lhs[n, pl.ds(TALL, TALL), :]).T

    @pl.loop(0, len(SLABS) + 1)
    def _(e):
        biasacc[e] = jnp.zeros((TALL, CHUNK), jnp.float32)

    score, weight = stages[:DEPTH], stages[DEPTH:]
    weight[0][...] = jnp.zeros((2 * TALL, WIDE), jnp.bfloat16)
    lanes = lax.broadcasted_iota(jnp.int32, (1, CHUNK), 1)
    places = [key_place(x, c, lanes) for c in range(3)]
    halves = (slice(0, CHUNK), slice(CHUNK, WIDE))

    def entry(k):
        chunks = [plan_ref[SLOTS + 2 * k + half] for half in range(2)]
        slabs = [plan_ref[3 * SLOTS + 2 * k + half] for half in range(2)]
        return plan_ref[k], chunks, slabs

    def scores(k, s):
        g, chunks, slabs = entry(k)
        for cols, n in zip(halves, chunks):
            s[:, cols] = lax.dot_general(
                lhs[g], line[chunk(n), :], NT, preferred_element_type=jnp.float32
            )

    def weigh(k, s, w_out):
        g, chunks, slabs = entry(k)
        for cols, n, e in zip(halves, chunks, slabs):
            pair = lax.div(n, 3)
            c = n - 3 * pair
            key = PAIR * pair + jnp.where(c == 0, places[0], jnp.where(c == 1, places[1], places[2]))
            half = s[pl.ds(0, TALL), cols] + table[e]
            half = jnp.where(key >= starts[g], half, LOW)
            t = jnp.tanh(half)
            u = 1.0 + t
            w = half * u
            ds = s[pl.ds(TALL, TALL), cols] * (u + w * (1.0 - t))
            biasacc[e] += ds
            w_out[pl.ds(0, TALL), cols] = w.astype(jnp.bfloat16)
            w_out[pl.ds(TALL, TALL), cols] = ds.astype(jnp.bfloat16)

    def gather(k, w_in):
        g, chunks, slabs = entry(k)
        keyvals = jnp.concatenate([line[chunk(n), :] for n in chunks], axis=0)
        od = jnp.dot(w_in[...], keyvals, preferred_element_type=jnp.float32)
        acc[g] += jnp.where(left, od[TALL:], od[:TALL])
        for rows, low in ((pl.ds(0, HD), TALL), (pl.ds(HD, HD), 0)):
            part = jnp.dot(
                qgt[g, rows, :], w_in[pl.ds(low, TALL), :], preferred_element_type=jnp.float32
            )
            for cols, n in zip(halves, chunks):
                dkv[n, rows, :] += part[:, cols]

    scores(1, score[1])

    @pl.loop(0, lax.div(plan_ref[5 * SLOTS] + DEPTH, DEPTH))
    def _(step):
        for i in range(DEPTH):
            k = DEPTH * step + i
            now, later = (i + 1) % DEPTH, (i + 2) % DEPTH
            gather(k, weight[i])
            weigh(k + 1, score[now], weight[now])
            scores(k + 2, score[later])

    @pl.loop(0, GROUPS)
    def _(n):
        for c in range(3):
            line[chunk(3 * n + c), :] = dkv[3 * n + c].astype(jnp.bfloat16).T
        acc[n] = acc[n] * scales[n]
        mine_ref[n] = acc[n, pl.ds(q_own, ROWS), :]
        theirs_ref[n] = acc[n, pl.ds(q_x, ROWS), :].astype(jnp.bfloat16)
        keep_ref[n, :ROWS] = line[block(n, k_own), :]
        keep_ref[n, ROWS:] = line[block(n, k_x), :]
        give_ref[n, :ROWS] = line[block(n, k_core), :]
        give_ref[n, ROWS:] = line[block(n, k_both), :]


def combine_kernel(mine_ref, got_qo_ref, dkv_ref, got_dkv_ref, out_ref):
    @pl.loop(0, GROUPS)
    def _(n):
        qo = mine_ref[n] + got_qo_ref[n].astype(jnp.float32)
        out_ref[n, :ROWS] = qo.astype(jnp.bfloat16)
        dkv = dkv_ref[n, :ROWS] + got_dkv_ref[n].astype(jnp.float32)
        out_ref[n, ROWS : 2 * ROWS] = dkv.astype(jnp.bfloat16)


def bias_kernel(in_ref, b0_ref, b1_ref, b2_ref, b3_ref, out_ref, terms_ref, sem):
    total = b0_ref[...] + b1_ref[...] + b2_ref[...] + b3_ref[...]
    high = total.astype(jnp.bfloat16)
    rest = total - high.astype(jnp.float32)
    middle = rest.astype(jnp.bfloat16)
    low = rest - middle.astype(jnp.float32)
    row = lax.broadcasted_iota(jnp.int32, (8, 128), 0)
    terms = jnp.where(
        row == 0,
        high.astype(jnp.float32),
        jnp.where(row == 1, middle.astype(jnp.float32), jnp.where(row == 2, low, 0.0)),
    )
    terms = jnp.concatenate([terms, jnp.zeros((8, 128), jnp.float32)], axis=0)
    for n in range(GROUPS):
        terms_ref[n] = terms.astype(jnp.bfloat16)
    copy = pltpu.make_async_copy(terms_ref, out_ref.at[:, pl.ds(2 * ROWS, 16), :], sem)
    copy.start()
    copy.wait()


def unpack_kernel(in_ref, out_ref, grad_ref):
    for h in range(0, H, 2):
        cols = slice(h * HD, (h + 2) * HD)
        a, b = in_ref[h, :ROWS], in_ref[h + 1, :ROWS]
        grad_ref[0, :, cols] = jnp.concatenate([a[:, :HD], b[:, :HD]], axis=1)
        out_ref[:, cols] = jnp.concatenate([a[:, HD:], b[:, HD:]], axis=1)
        a, b = in_ref[h, ROWS : 2 * ROWS], in_ref[h + 1, ROWS : 2 * ROWS]
        grad_ref[1, :, cols] = jnp.concatenate([a[:, :HD], b[:, :HD]], axis=1)
        grad_ref[2, :, cols] = jnp.concatenate([a[:, HD:], b[:, HD:]], axis=1)


def swap(v, axis, partner):
    return lax.ppermute(v, axis, [(i, p) for i, p in enumerate(partner)])


def per_device(qkv, grad_out, rab, doc_ids):
    bf16, f32 = jnp.bfloat16, jnp.float32
    x, y, z, core = (lax.axis_index(a) for a in ("x", "y", "z", "core"))
    whole = pl.BlockSpec(memory_space=VMEM)
    scalars = pl.BlockSpec(memory_space=SMEM)
    block = jax.ShapeDtypeStruct((H, ROWS, 128), bf16)
    double = jax.ShapeDtypeStruct((H, 2 * ROWS, 128), bf16)
    slabs = jax.ShapeDtypeStruct((len(SLABS) + 1, TALL, CHUNK), f32)
    small = pltpu.CompilerParams(vmem_limit_bytes=8 * 2**20)
    large = pltpu.CompilerParams(vmem_limit_bytes=34 * 2**20)
    first_row = (((y * 4 + z) * 2 + core) * 4 + x) * ROWS
    where = jnp.stack([x, core])
    packed, bounds = pl.pallas_call(
        pack_kernel,
        out_shape=(double, jax.ShapeDtypeStruct((DOCS,), jnp.int32)),
        in_specs=[scalars] + [pl.BlockSpec(memory_space=pltpu.HBM)] * 3,
        out_specs=(whole, scalars),
        scratch_shapes=[
            VMEM((96, 128), jnp.int32),
            VMEM((3, ROWS, H * HD), bf16),
            VMEM((ROWS, H * HD), bf16),
            pltpu.SemaphoreType.DMA((3,)),
        ],
        compiler_params=pltpu.CompilerParams(vmem_limit_bytes=63 * 2**20),
        name="pack",
    )(first_row.reshape(1), doc_ids.reshape(96, 128), qkv.transpose(1, 0, 2), grad_out)
    own = lax.all_to_all(packed, ("y", "z"), 0, 0, tiled=True)
    kv_own, qg_own = own[:, :ROWS], own[:, ROWS:]
    kv_x = swap(kv_own, "x", (1, 0, 3, 2))
    qg_x = swap(qg_own, "x", (3, 2, 1, 0))
    kv_core = swap(kv_own, "core", (1, 0))
    table_row = lax.dynamic_slice_in_dim(rab, y * 4 + z, 1, 0)[0]
    table, starts, scales, plan = pl.pallas_call(
        table_kernel,
        out_shape=(
            slabs,
            jax.ShapeDtypeStruct((GROUPS, TALL, 128), jnp.int32),
            jax.ShapeDtypeStruct((GROUPS, TALL, 128), f32),
            jax.ShapeDtypeStruct((5 * SLOTS + 1,), jnp.int32),
        ),
        in_specs=[scalars] * 3,
        out_specs=(whole, whole, whole, scalars),
        compiler_params=small,
        cost_estimate=pl.CostEstimate(flops=0, bytes_accessed=0, transcendentals=0),
        name="table",
    )(where, table_row, bounds)
    kv_x, qg_x, table, starts, scales, plan = lax.optimization_barrier(
        (kv_x, qg_x, table, starts, scales, plan)
    )
    kv_both = swap(kv_x, "core", (1, 0))
    keep, give, mine, theirs, sums = pl.pallas_call(
        main_kernel,
        out_shape=[double, double, jax.ShapeDtypeStruct((H, ROWS, 128), f32), block, slabs],
        in_specs=[scalars] * 2 + [whole] * 8,
        out_specs=[whole] * 5,
        scratch_shapes=[
            VMEM((GROUPS * SUPER, 128), bf16),
            VMEM((3 * GROUPS, 128, CHUNK), f32),
            VMEM((GROUPS, TALL, 128), f32),
            VMEM((GROUPS, 2 * TALL, 128), bf16),
            VMEM((GROUPS, 128, TALL), bf16),
        ]
        + [VMEM((2 * TALL, WIDE), f32)] * DEPTH
        + [VMEM((2 * TALL, WIDE), bf16)] * DEPTH,
        compiler_params=large,
        name="attend",
    )(where, plan, table, starts, scales, own, kv_x, kv_core, kv_both, qg_x)
    got = swap(give, "core", (1, 0))
    dkv = keep.astype(f32) + got.astype(f32)
    dkv_x = dkv[:, ROWS:].astype(bf16)
    got_qo = swap(theirs, "x", (3, 2, 1, 0))
    got_dkv = swap(dkv_x, "x", (1, 0, 3, 2))
    bias = pl.pallas_call(
        buckets_kernel,
        out_shape=jax.ShapeDtypeStruct((8, 128), f32),
        in_specs=[scalars, whole],
        out_specs=whole,
        scratch_shapes=[VMEM((NB, 8, 128), f32)],
        compiler_params=small,
        cost_estimate=pl.CostEstimate(flops=0, bytes_accessed=0, transcendentals=0),
        name="buckets",
    )(where, sums)
    others = [swap(bias, "x", p) for p in ((1, 0, 3, 2), (3, 2, 1, 0), (2, 3, 0, 1))]
    results = pl.pallas_call(
        combine_kernel,
        out_shape=jax.ShapeDtypeStruct((H, 2 * ROWS + 16, 128), bf16),
        in_specs=[whole] * 4,
        out_specs=whole,
        compiler_params=small,
        cost_estimate=pl.CostEstimate(flops=0, bytes_accessed=10**7, transcendentals=0),
        name="combine",
    )(mine, got_qo, dkv, got_dkv)
    results = pl.pallas_call(
        bias_kernel,
        out_shape=jax.ShapeDtypeStruct((H, 2 * ROWS + 16, 128), bf16),
        in_specs=[pl.BlockSpec(memory_space=pl.ANY)] + [whole] * 4,
        out_specs=pl.BlockSpec(memory_space=pl.ANY),
        scratch_shapes=[VMEM((GROUPS, 16, 128), bf16), pltpu.SemaphoreType.DMA(())],
        input_output_aliases={0: 0},
        compiler_params=small,
        name="bias",
    )(results, bias, *others)
    results = lax.all_to_all(results, ("y", "z"), 0, 0, tiled=True)
    terms = lax.dynamic_slice(results, (x * 4, 2 * ROWS, 0), (4, 3, NB)).astype(f32)
    bias_grad = terms[:, 0] + terms[:, 1] + terms[:, 2]
    bias_grad = bias_grad + swap(bias_grad, "core", (1, 0))
    out, grad_qkv = pl.pallas_call(
        unpack_kernel,
        out_shape=(
            jax.ShapeDtypeStruct((ROWS, H * HD), bf16),
            jax.ShapeDtypeStruct((3, ROWS, H * HD), bf16),
        ),
        in_specs=[whole],
        out_specs=(whole, whole),
        compiler_params=small,
        name="unpack",
    )(results)
    return out, grad_qkv.transpose(1, 0, 2), bias_grad


def solution(mesh):
    fine = Mesh(mesh.devices.reshape(4, 4, 4, 2), ("x", "y", "z", "core"))
    rows = ("y", "z", "core", "x")
    return jax.shard_map(
        per_device,
        mesh=fine,
        in_specs=(P(rows, None, None), P(rows, None), P(), P()),
        out_specs=(P(rows, None), P(rows, None, None), P("x", None)),
        check_vma=False,
    )
```

```python
import jax
import jax.numpy as jnp
from jax import lax
from jax.experimental import pallas as pl
from jax.experimental.pallas import tpu as pltpu
from jax.sharding import Mesh
from jax.sharding import PartitionSpec as P

HD = 64
H = 16
NB = 20
DOCS = 8
ROWS = 96
SUPER = 384
GROUPS = 16
PAIR = 768
TALL = 192
WIDE = 256
CHUNK = 128
SLOTS = 256
DEPTH = 6
LOW = -1e30
VMEM = pltpu.VMEM
SMEM = pltpu.SMEM
NT = (((1,), (1,)), ((), ()))


def doc_bounds(ids):
    return [jnp.int32(0)] + [
        jnp.sum((ids < d).astype(jnp.float32)).astype(jnp.int32) for d in range(1, DOCS)
    ]


def pack_kernel(where_ref, ids, qkv, g_in, out_ref, bounds_ref, ids_ref, qkv_ref, g_ref, sems):
    copies = [
        pltpu.make_async_copy(source, target, sems.at[k])
        for k, (source, target) in enumerate(((ids, ids_ref), (qkv, qkv_ref), (g_in, g_ref)))
    ]
    for copy in copies:
        copy.start()
    copies[0].wait()
    bounds = doc_bounds(ids_ref[...])
    for d in range(DOCS):
        bounds_ref[d] = bounds[d]
    pos = where_ref[0] + lax.broadcasted_iota(jnp.int32, (ROWS, 128), 0)
    length = jnp.zeros((ROWS, 128), jnp.int32)
    ends = bounds[1:] + [jnp.int32(PAIR * GROUPS)]
    for d in range(DOCS):
        length = jnp.where(pos >= bounds[d], ends[d] - bounds[d], length)
    scale = lax.rsqrt(length.astype(jnp.float32))[:, :HD]
    copies[1].wait()
    copies[2].wait()
    for h in range(H):
        cols = slice(h * HD, (h + 1) * HD)
        out_ref[h, :ROWS] = jnp.concatenate([qkv_ref[1, :, cols], qkv_ref[2, :, cols]], axis=1)
        q = (qkv_ref[0, :, cols].astype(jnp.float32) * 0.0625).astype(jnp.bfloat16)
        g = (g_ref[:, cols].astype(jnp.float32) * scale).astype(jnp.bfloat16)
        out_ref[h, ROWS:] = jnp.concatenate([q, g], axis=1)


EDGES = [(k, k) for k in range(8)] + [(2**p, p + 6) for p in range(3, 13)]


def edges_of(low, high):
    below = [edge for edge in EDGES if edge[0] <= low]
    return below[-1:], [edge for edge in EDGES if low < edge[0] <= high]


def key_place(x, c, lane):
    j = CHUNK * c + lane
    return j + 2 * ROWS * lax.div(x, 2) + jnp.where(j >= 2 * ROWS, SUPER - 2 * ROWS, 0)


SLABS = [
    (c, e, PAIR * e - (319, 639, 767)[c], PAIR * e + PAIR - 1 - (0, 128, 448)[c])
    for c in range(3)
    for e in range(9)
]


def distance(x, core, c, row):
    i = row + lax.broadcasted_iota(jnp.int32, (16, CHUNK), 0)
    lane = lax.broadcasted_iota(jnp.int32, (16, CHUNK), 1)
    lower = jnp.minimum(x, 3 - x)
    i = i + ROWS * lower + jnp.where(i >= ROWS, ROWS * (2 - 2 * lower), 0)
    return SUPER * core + i - key_place(x, c, lane)


def start_of(bounds_ref, pos):
    start = jnp.int32(0)
    for d in range(1, DOCS):
        start = jnp.where(pos >= bounds_ref[d], bounds_ref[d], start)
    return start


def span_of(x, core, g):
    lower = jnp.minimum(x, 3 - x)
    base = PAIR * g + SUPER * core
    return base + ROWS * lower, base + ROWS * (4 - lower) - 1


def table_kernel(where_ref, rab_ref, bounds_ref, table_ref, starts_ref, scales_ref, plan_ref):
    x, core = where_ref[0], where_ref[1]
    column = 2 * ROWS * lax.div(x, 2)

    def of_group(g, at):
        first, last = span_of(x, core, g)
        begin = start_of(bounds_ref, first)

        def of_pair(n, at):
            for c, (low, high) in enumerate(((0, 127), (128, 447), (448, 575))):
                place = PAIR * n + column
                live = (place + high >= begin) & (place + low <= last)
                plan_ref[lax.div(at, 2)] = g
                plan_ref[SLOTS + at] = 3 * n + c
                plan_ref[3 * SLOTS + at] = 9 * c + g - n + 1
                at = at + live.astype(jnp.int32)
            return at

        at = lax.fori_loop(lax.div(begin, PAIR), g + 1, of_pair, at)
        plan_ref[SLOTS + at] = 0
        plan_ref[3 * SLOTS + at] = 0
        return at + lax.rem(at, 2)

    at = lax.fori_loop(0, GROUPS, of_group, jnp.int32(2))
    tiles = lax.div(at, 2)
    plan_ref[5 * SLOTS] = tiles - 1
    plan_ref[0] = 0
    for extra in range(DEPTH + 1):
        plan_ref[tiles + extra] = 0
    for half in range(2):
        plan_ref[SLOTS + half] = 0
        plan_ref[3 * SLOTS + half] = 0
        for extra in range(DEPTH + 1):
            plan_ref[SLOTS + at + 2 * extra + half] = 0
            plan_ref[3 * SLOTS + at + 2 * extra + half] = 0

    table_ref[0] = jnp.full((TALL, CHUNK), LOW, jnp.float32)

    @pl.loop(0, TALL // 16)
    def _(step):
        row = pl.multiple_of(step * 16, 16)
        near = [distance(x, core, c, row) for c in range(3)]
        for index, (c, e, low, high) in enumerate(SLABS):
            below, inside = edges_of(low, high)
            value = jnp.full((16, CHUNK), rab_ref[below[0][1]] * 0.5 if below else LOW, jnp.float32)
            for edge, b in inside:
                value = jnp.where(near[c] >= edge - PAIR * e, rab_ref[b] * 0.5, value)
            table_ref[index + 1, pl.ds(row, 16), :] = value

    left = lax.broadcasted_iota(jnp.int32, (TALL, 128), 1) < HD
    row = lax.broadcasted_iota(jnp.int32, (TALL, 128), 0)
    offset = row + jnp.where(row >= ROWS, ROWS * (2 - 2 * jnp.minimum(x, 3 - x)), 0)

    @pl.loop(0, GROUPS)
    def _(g):
        first, last = span_of(x, core, g)
        pos = first + offset
        d_first, d_last = jnp.int32(0), jnp.int32(0)
        for d in range(1, DOCS):
            d_first = d_first + (first >= bounds_ref[d]).astype(jnp.int32)
            d_last = d_last + (last >= bounds_ref[d]).astype(jnp.int32)
        starts_ref[g] = jnp.zeros((TALL, 128), jnp.int32)
        scales_ref[g] = jnp.zeros((TALL, 128), jnp.float32)

        def history(d, carry):
            begin = bounds_ref[d]
            end = jnp.where(d + 1 < DOCS, bounds_ref[jnp.minimum(d + 1, DOCS - 1)], PAIR * GROUPS)
            inside = pos >= begin
            size = jnp.full((TALL, 128), end - begin, jnp.int32).astype(jnp.float32)
            starts_ref[g] = jnp.where(inside, begin, starts_ref[g])
            scales_ref[g] = jnp.where(
                left, 0.0625, jnp.where(inside, lax.rsqrt(size), scales_ref[g])
            )
            return carry

        lax.fori_loop(d_first, d_last + 1, history, 0)


def buckets_kernel(where_ref, sums_ref, bias_ref, buckets):
    x, core = where_ref[0], where_ref[1]
    buckets[...] = jnp.zeros((NB, 8, 128), jnp.float32)

    @pl.loop(0, TALL // 16)
    def _(step):
        row = pl.multiple_of(step * 16, 16)
        near = [distance(x, core, c, row) for c in range(3)]
        totals = [jnp.zeros((8, 128), jnp.float32)] * NB
        for index, (c, e, low, high) in enumerate(SLABS):
            below, inside = edges_of(low, high)
            v = sums_ref[index + 1, pl.ds(row, 16), :]
            found = [(b, v[:8] + v[8:]) for edge, b in below]
            for edge, b in inside:
                part = jnp.where(near[c] >= edge - PAIR * e, v, 0.0)
                found.append((b, part[:8] + part[8:]))
            for k, (b, total) in enumerate(found):
                totals[b] = totals[b] + total
                if k:
                    totals[found[k - 1][0]] = totals[found[k - 1][0]] - total
        for b in range(NB):
            buckets[b] += totals[b]

    lane = lax.broadcasted_iota(jnp.int32, (8, 128), 1)
    row = jnp.zeros((8, 128), jnp.float32)
    for b in range(NB):
        total = jnp.sum(jnp.sum(buckets[b], axis=0, keepdims=True), axis=1, keepdims=True)
        row = jnp.where(lane == b, total * 0.5, row)
    bias_ref[...] = row


def main_kernel(
    where_ref, plan_ref, table, starts, scales, own_ref, kvx_ref, kvc_ref, kvxc_ref, qgx_ref,
    keep_ref, give_ref, mine_ref, theirs_ref, biasacc,
    line, dkv, acc, lhs, qgt, *stages,
):
    x = where_ref[0]
    core = where_ref[1]
    odd = lax.rem(x, 2)
    lower = jnp.minimum(x, 3 - x)

    def aligned(v):
        return pl.multiple_of(v * ROWS, ROWS)

    k_own = aligned(2 * core + odd)
    k_x = aligned(2 * core + 1 - odd)
    k_core = aligned(2 * (1 - core) + odd)
    k_both = aligned(2 * (1 - core) + 1 - odd)
    q_own = aligned((x != lower).astype(jnp.int32))
    q_x = aligned((x == lower).astype(jnp.int32))
    lane = lax.broadcasted_iota(jnp.int32, (TALL, 128), 1)
    left = lane < HD

    def chunk(k):
        return pl.ds(pl.multiple_of(CHUNK * k, CHUNK), CHUNK)

    def block(n, at):
        return pl.ds(pl.multiple_of(SUPER * n + at, ROWS), ROWS)

    @pl.loop(0, GROUPS, unroll=8)
    def _(n):
        line[block(n, k_own), :] = own_ref[n, :ROWS]
        line[block(n, k_x), :] = kvx_ref[n]
        line[block(n, k_core), :] = kvc_ref[n]
        line[block(n, k_both), :] = kvxc_ref[n]
        for c in range(3):
            dkv[3 * n + c] = jnp.zeros((128, CHUNK), jnp.float32)
        acc[n] = jnp.zeros((TALL, 128), jnp.float32)
        zero = jnp.zeros((ROWS, 128), jnp.bfloat16)
        for at, qg in ((q_own, own_ref[n, ROWS:]), (q_x, qgx_ref[n])):
            lhs[n, pl.ds(at, ROWS), :] = jnp.where(left[:ROWS], qg, zero)
            lhs[n, pl.ds(pl.multiple_of(at + TALL, ROWS), ROWS), :] = jnp.where(left[:ROWS], zero, qg)
        qgt[n] = (lhs[n, pl.ds(0, TALL), :] + lhs[n, pl.ds(TALL, TALL), :]).T

    @pl.loop(0, len(SLABS) + 1, unroll=7)
    def _(e):
        biasacc[e] = jnp.zeros((TALL, CHUNK), jnp.float32)

    score, weight = stages[:DEPTH], stages[DEPTH:]
    weight[0][...] = jnp.zeros((2 * TALL, WIDE), jnp.bfloat16)
    lanes = lax.broadcasted_iota(jnp.int32, (1, CHUNK), 1)
    places = [key_place(x, c, lanes) for c in range(3)]
    halves = (slice(0, CHUNK), slice(CHUNK, WIDE))

    def entry(k):
        chunks = [plan_ref[SLOTS + 2 * k + half] for half in range(2)]
        slabs = [plan_ref[3 * SLOTS + 2 * k + half] for half in range(2)]
        return plan_ref[k], chunks, slabs

    def scores(k, s):
        g, chunks, slabs = entry(k)
        for cols, n in zip(halves, chunks):
            s[:, cols] = lax.dot_general(
                lhs[g], line[chunk(n), :], NT, preferred_element_type=jnp.float32
            )

    def weigh(k, s, w_out):
        g, chunks, slabs = entry(k)
        for cols, n, e in zip(halves, chunks, slabs):
            pair = lax.div(n, 3)
            c = n - 3 * pair
            key = PAIR * pair + jnp.where(c == 0, places[0], jnp.where(c == 1, places[1], places[2]))
            half = s[pl.ds(0, TALL), cols] + table[e]
            half = jnp.where(key >= starts[g], half, LOW)
            t = jnp.tanh(half)
            u = 1.0 + t
            w = half * u
            ds = s[pl.ds(TALL, TALL), cols] * (u + w * (1.0 - t))
            biasacc[e] += ds
            w_out[pl.ds(0, TALL), cols] = w.astype(jnp.bfloat16)
            w_out[pl.ds(TALL, TALL), cols] = ds.astype(jnp.bfloat16)

    def gather(k, w_in):
        g, chunks, slabs = entry(k)
        keyvals = jnp.concatenate([line[chunk(n), :] for n in chunks], axis=0)
        od = jnp.dot(w_in[...], keyvals, preferred_element_type=jnp.float32)
        acc[g] += jnp.where(left, od[TALL:], od[:TALL])
        for rows, low in ((pl.ds(0, HD), TALL), (pl.ds(HD, HD), 0)):
            part = jnp.dot(
                qgt[g, rows, :], w_in[pl.ds(low, TALL), :], preferred_element_type=jnp.float32
            )
            for cols, n in zip(halves, chunks):
                dkv[n, rows, :] += part[:, cols]

    scores(1, score[1])

    @pl.loop(0, lax.div(plan_ref[5 * SLOTS] + DEPTH, DEPTH))
    def _(step):
        for i in range(DEPTH):
            k = DEPTH * step + i
            now, later = (i + 1) % DEPTH, (i + 2) % DEPTH
            gather(k, weight[i])
            weigh(k + 1, score[now], weight[now])
            scores(k + 2, score[later])

    @pl.loop(0, GROUPS, unroll=4)
    def _(n):
        for c in range(3):
            line[chunk(3 * n + c), :] = dkv[3 * n + c].astype(jnp.bfloat16).T
        acc[n] = acc[n] * scales[n]
        mine_ref[n] = acc[n, pl.ds(q_own, ROWS), :]
        theirs_ref[n] = acc[n, pl.ds(q_x, ROWS), :].astype(jnp.bfloat16)
        keep_ref[n, :ROWS] = line[block(n, k_own), :]
        keep_ref[n, ROWS:] = line[block(n, k_x), :]
        give_ref[n, :ROWS] = line[block(n, k_core), :]
        give_ref[n, ROWS:] = line[block(n, k_both), :]


def combine_kernel(mine_ref, got_qo_ref, dkv_ref, got_dkv_ref, out_ref):
    @pl.loop(0, GROUPS, unroll=4)
    def _(n):
        qo = mine_ref[n] + got_qo_ref[n].astype(jnp.float32)
        out_ref[n, :ROWS] = qo.astype(jnp.bfloat16)
        dkv = dkv_ref[n, :ROWS] + got_dkv_ref[n].astype(jnp.float32)
        out_ref[n, ROWS : 2 * ROWS] = dkv.astype(jnp.bfloat16)


def bias_kernel(in_ref, b0_ref, b1_ref, b2_ref, b3_ref, out_ref, terms_ref, sem):
    total = b0_ref[...] + b1_ref[...] + b2_ref[...] + b3_ref[...]
    high = total.astype(jnp.bfloat16)
    rest = total - high.astype(jnp.float32)
    middle = rest.astype(jnp.bfloat16)
    low = rest - middle.astype(jnp.float32)
    row = lax.broadcasted_iota(jnp.int32, (8, 128), 0)
    terms = jnp.where(
        row == 0,
        high.astype(jnp.float32),
        jnp.where(row == 1, middle.astype(jnp.float32), jnp.where(row == 2, low, 0.0)),
    )
    terms = jnp.concatenate([terms, jnp.zeros((8, 128), jnp.float32)], axis=0)
    for n in range(GROUPS):
        terms_ref[n] = terms.astype(jnp.bfloat16)
    copy = pltpu.make_async_copy(terms_ref, out_ref.at[:, pl.ds(2 * ROWS, 16), :], sem)
    copy.start()
    copy.wait()


def unpack_kernel(in_ref, out_ref, grad_ref):
    for h in range(0, H, 2):
        cols = slice(h * HD, (h + 2) * HD)
        a, b = in_ref[h, :ROWS], in_ref[h + 1, :ROWS]
        grad_ref[0, :, cols] = jnp.concatenate([a[:, :HD], b[:, :HD]], axis=1)
        out_ref[:, cols] = jnp.concatenate([a[:, HD:], b[:, HD:]], axis=1)
        a, b = in_ref[h, ROWS : 2 * ROWS], in_ref[h + 1, ROWS : 2 * ROWS]
        grad_ref[1, :, cols] = jnp.concatenate([a[:, :HD], b[:, :HD]], axis=1)
        grad_ref[2, :, cols] = jnp.concatenate([a[:, HD:], b[:, HD:]], axis=1)


def swap(v, axis, partner):
    return lax.ppermute(v, axis, [(i, p) for i, p in enumerate(partner)])


def per_device(qkv, grad_out, rab, doc_ids):
    bf16, f32 = jnp.bfloat16, jnp.float32
    x, y, z, core = (lax.axis_index(a) for a in ("x", "y", "z", "core"))
    whole = pl.BlockSpec(memory_space=VMEM)
    scalars = pl.BlockSpec(memory_space=SMEM)
    block = jax.ShapeDtypeStruct((H, ROWS, 128), bf16)
    double = jax.ShapeDtypeStruct((H, 2 * ROWS, 128), bf16)
    slabs = jax.ShapeDtypeStruct((len(SLABS) + 1, TALL, CHUNK), f32)
    small = pltpu.CompilerParams(vmem_limit_bytes=8 * 2**20)
    large = pltpu.CompilerParams(vmem_limit_bytes=34 * 2**20)
    first_row = (((y * 4 + z) * 2 + core) * 4 + x) * ROWS
    where = jnp.stack([x, core])
    packed, bounds = pl.pallas_call(
        pack_kernel,
        out_shape=(double, jax.ShapeDtypeStruct((DOCS,), jnp.int32)),
        in_specs=[scalars] + [pl.BlockSpec(memory_space=pltpu.HBM)] * 3,
        out_specs=(whole, scalars),
        scratch_shapes=[
            VMEM((96, 128), jnp.int32),
            VMEM((3, ROWS, H * HD), bf16),
            VMEM((ROWS, H * HD), bf16),
            pltpu.SemaphoreType.DMA((3,)),
        ],
        compiler_params=pltpu.CompilerParams(vmem_limit_bytes=63 * 2**20),
        name="pack",
    )(first_row.reshape(1), doc_ids.reshape(96, 128), qkv.transpose(1, 0, 2), grad_out)
    own = lax.all_to_all(packed, ("y", "z"), 0, 0, tiled=True)
    kv_own, qg_own = own[:, :ROWS], own[:, ROWS:]
    qg_x = swap(qg_own, "x", (3, 2, 1, 0))
    kv_x = swap(kv_own, "x", (1, 0, 3, 2))
    kv_core = swap(kv_own, "core", (1, 0))
    table_row = lax.dynamic_slice_in_dim(rab, y * 4 + z, 1, 0)[0]
    table, starts, scales, plan = pl.pallas_call(
        table_kernel,
        out_shape=(
            slabs,
            jax.ShapeDtypeStruct((GROUPS, TALL, 128), jnp.int32),
            jax.ShapeDtypeStruct((GROUPS, TALL, 128), f32),
            jax.ShapeDtypeStruct((5 * SLOTS + 1,), jnp.int32),
        ),
        in_specs=[scalars] * 3,
        out_specs=(whole, whole, whole, scalars),
        compiler_params=small,
        cost_estimate=pl.CostEstimate(flops=0, bytes_accessed=0, transcendentals=0),
        name="table",
    )(where, table_row, bounds)
    kv_x, qg_x, table, starts, scales, plan = lax.optimization_barrier(
        (kv_x, qg_x, table, starts, scales, plan)
    )
    kv_both = swap(kv_x, "core", (1, 0))
    keep, give, mine, theirs, sums = pl.pallas_call(
        main_kernel,
        out_shape=[double, double, jax.ShapeDtypeStruct((H, ROWS, 128), f32), block, slabs],
        in_specs=[scalars] * 2 + [whole] * 8,
        out_specs=[whole] * 5,
        scratch_shapes=[
            VMEM((GROUPS * SUPER, 128), bf16),
            VMEM((3 * GROUPS, 128, CHUNK), f32),
            VMEM((GROUPS, TALL, 128), f32),
            VMEM((GROUPS, 2 * TALL, 128), bf16),
            VMEM((GROUPS, 128, TALL), bf16),
        ]
        + [VMEM((2 * TALL, WIDE), f32)] * DEPTH
        + [VMEM((2 * TALL, WIDE), bf16)] * DEPTH,
        compiler_params=large,
        name="attend",
    )(where, plan, table, starts, scales, own, kv_x, kv_core, kv_both, qg_x)
    got = swap(give, "core", (1, 0))
    dkv = keep.astype(f32) + got.astype(f32)
    dkv_x = dkv[:, ROWS:].astype(bf16)
    got_qo = swap(theirs, "x", (3, 2, 1, 0))
    got_dkv = swap(dkv_x, "x", (1, 0, 3, 2))
    bias = pl.pallas_call(
        buckets_kernel,
        out_shape=jax.ShapeDtypeStruct((8, 128), f32),
        in_specs=[scalars, whole],
        out_specs=whole,
        scratch_shapes=[VMEM((NB, 8, 128), f32)],
        compiler_params=small,
        cost_estimate=pl.CostEstimate(flops=0, bytes_accessed=0, transcendentals=0),
        name="buckets",
    )(where, sums)
    others = [swap(bias, "x", p) for p in ((1, 0, 3, 2), (3, 2, 1, 0), (2, 3, 0, 1))]
    results = pl.pallas_call(
        combine_kernel,
        out_shape=jax.ShapeDtypeStruct((H, 2 * ROWS + 16, 128), bf16),
        in_specs=[whole] * 4,
        out_specs=whole,
        compiler_params=small,
        cost_estimate=pl.CostEstimate(flops=0, bytes_accessed=10**7, transcendentals=0),
        name="combine",
    )(mine, got_qo, dkv, got_dkv)
    results = pl.pallas_call(
        bias_kernel,
        out_shape=jax.ShapeDtypeStruct((H, 2 * ROWS + 16, 128), bf16),
        in_specs=[pl.BlockSpec(memory_space=pl.ANY)] + [whole] * 4,
        out_specs=pl.BlockSpec(memory_space=pl.ANY),
        scratch_shapes=[VMEM((GROUPS, 16, 128), bf16), pltpu.SemaphoreType.DMA(())],
        input_output_aliases={0: 0},
        compiler_params=small,
        name="bias",
    )(results, bias, *others)
    results = lax.all_to_all(results, ("y", "z"), 0, 0, tiled=True)
    terms = lax.dynamic_slice(results, (x * 4, 2 * ROWS, 0), (4, 3, NB)).astype(f32)
    bias_grad = terms[:, 0] + terms[:, 1] + terms[:, 2]
    bias_grad = bias_grad + swap(bias_grad, "core", (1, 0))
    out, grad_qkv = pl.pallas_call(
        unpack_kernel,
        out_shape=(
            jax.ShapeDtypeStruct((ROWS, H * HD), bf16),
            jax.ShapeDtypeStruct((3, ROWS, H * HD), bf16),
        ),
        in_specs=[whole],
        out_specs=(whole, whole),
        compiler_params=small,
        name="unpack",
    )(results)
    return out, grad_qkv.transpose(1, 0, 2), bias_grad


def solution(mesh):
    fine = Mesh(mesh.devices.reshape(4, 4, 4, 2), ("x", "y", "z", "core"))
    rows = ("y", "z", "core", "x")
    return jax.shard_map(
        per_device,
        mesh=fine,
        in_specs=(P(rows, None, None), P(rows, None), P(), P()),
        out_specs=(P(rows, None), P(rows, None, None), P("x", None)),
        check_vma=False,
    )
```

```python
import jax
import jax.numpy as jnp
from jax import lax
from jax.experimental import pallas as pl
from jax.experimental.pallas import tpu as pltpu
from jax.sharding import Mesh
from jax.sharding import PartitionSpec as P

HD = 64
H = 16
NB = 20
DOCS = 8
ROWS = 96
SUPER = 384
GROUPS = 16
PAIR = 768
TALL = 192
WIDE = 256
CHUNK = 128
SLOTS = 256
DEPTH = 6
LOW = -1e30
VMEM = pltpu.VMEM
SMEM = pltpu.SMEM
NT = (((1,), (1,)), ((), ()))


def doc_bounds(ids):
    return [jnp.int32(0)] + [
        jnp.sum((ids < d).astype(jnp.float32)).astype(jnp.int32) for d in range(1, DOCS)
    ]


def pack_kernel(where_ref, ids, qkv, g_in, out_ref, bounds_ref, ids_ref, qkv_ref, g_ref, sems):
    copies = [
        pltpu.make_async_copy(source, target, sems.at[k])
        for k, (source, target) in enumerate(((ids, ids_ref), (qkv, qkv_ref), (g_in, g_ref)))
    ]
    for copy in copies:
        copy.start()
    copies[0].wait()
    bounds = doc_bounds(ids_ref[...])
    for d in range(DOCS):
        bounds_ref[d] = bounds[d]
    pos = where_ref[0] + lax.broadcasted_iota(jnp.int32, (ROWS, 128), 0)
    length = jnp.zeros((ROWS, 128), jnp.int32)
    ends = bounds[1:] + [jnp.int32(PAIR * GROUPS)]
    for d in range(DOCS):
        length = jnp.where(pos >= bounds[d], ends[d] - bounds[d], length)
    scale = lax.rsqrt(length.astype(jnp.float32))[:, :HD]
    copies[1].wait()
    copies[2].wait()
    for h in range(H):
        cols = slice(h * HD, (h + 1) * HD)
        out_ref[h, :ROWS] = jnp.concatenate([qkv_ref[1, :, cols], qkv_ref[2, :, cols]], axis=1)
        q = (qkv_ref[0, :, cols].astype(jnp.float32) * 0.0625).astype(jnp.bfloat16)
        g = (g_ref[:, cols].astype(jnp.float32) * scale).astype(jnp.bfloat16)
        out_ref[h, ROWS:] = jnp.concatenate([q, g], axis=1)


EDGES = [(k, k) for k in range(8)] + [(2**p, p + 6) for p in range(3, 13)]


def edges_of(low, high):
    below = [edge for edge in EDGES if edge[0] <= low]
    return below[-1:], [edge for edge in EDGES if low < edge[0] <= high]


def key_place(x, c, lane):
    j = CHUNK * c + lane
    return j + 2 * ROWS * lax.div(x, 2) + jnp.where(j >= 2 * ROWS, SUPER - 2 * ROWS, 0)


SLABS = [
    (c, e, PAIR * e - (319, 639, 767)[c], PAIR * e + PAIR - 1 - (0, 128, 448)[c])
    for c in range(3)
    for e in range(9)
]


def distance(x, core, c, row):
    i = row + lax.broadcasted_iota(jnp.int32, (16, CHUNK), 0)
    lane = lax.broadcasted_iota(jnp.int32, (16, CHUNK), 1)
    lower = jnp.minimum(x, 3 - x)
    i = i + ROWS * lower + jnp.where(i >= ROWS, ROWS * (2 - 2 * lower), 0)
    return SUPER * core + i - key_place(x, c, lane)


def start_of(bounds_ref, pos):
    start = jnp.int32(0)
    for d in range(1, DOCS):
        start = jnp.where(pos >= bounds_ref[d], bounds_ref[d], start)
    return start


def span_of(x, core, g):
    lower = jnp.minimum(x, 3 - x)
    base = PAIR * g + SUPER * core
    return base + ROWS * lower, base + ROWS * (4 - lower) - 1


def table_kernel(where_ref, rab_ref, bounds_ref, table_ref, starts_ref, scales_ref, plan_ref):
    x, core = where_ref[0], where_ref[1]
    column = 2 * ROWS * lax.div(x, 2)

    def of_group(g, at):
        first, last = span_of(x, core, g)
        begin = start_of(bounds_ref, first)

        def of_pair(n, at):
            for c, (low, high) in enumerate(((0, 127), (128, 447), (448, 575))):
                place = PAIR * n + column
                live = (place + high >= begin) & (place + low <= last)
                plan_ref[lax.div(at, 2)] = g
                plan_ref[SLOTS + at] = 3 * n + c
                plan_ref[3 * SLOTS + at] = 9 * c + g - n + 1
                at = at + live.astype(jnp.int32)
            return at

        at = lax.fori_loop(lax.div(begin, PAIR), g + 1, of_pair, at)
        plan_ref[SLOTS + at] = 0
        plan_ref[3 * SLOTS + at] = 0
        return at + lax.rem(at, 2)

    at = lax.fori_loop(0, GROUPS, of_group, jnp.int32(2))
    tiles = lax.div(at, 2)
    plan_ref[5 * SLOTS] = tiles - 1
    plan_ref[0] = 0
    for extra in range(DEPTH + 1):
        plan_ref[tiles + extra] = 0
    for half in range(2):
        plan_ref[SLOTS + half] = 0
        plan_ref[3 * SLOTS + half] = 0
        for extra in range(DEPTH + 1):
            plan_ref[SLOTS + at + 2 * extra + half] = 0
            plan_ref[3 * SLOTS + at + 2 * extra + half] = 0

    table_ref[0] = jnp.full((TALL, CHUNK), LOW, jnp.float32)

    @pl.loop(0, TALL // 16)
    def _(step):
        row = pl.multiple_of(step * 16, 16)
        near = [distance(x, core, c, row) for c in range(3)]
        for index, (c, e, low, high) in enumerate(SLABS):
            below, inside = edges_of(low, high)
            value = jnp.full((16, CHUNK), rab_ref[below[0][1]] * 0.5 if below else LOW, jnp.float32)
            for edge, b in inside:
                value = jnp.where(near[c] >= edge - PAIR * e, rab_ref[b] * 0.5, value)
            table_ref[index + 1, pl.ds(row, 16), :] = value

    left = lax.broadcasted_iota(jnp.int32, (TALL, 128), 1) < HD
    row = lax.broadcasted_iota(jnp.int32, (TALL, 128), 0)
    offset = row + jnp.where(row >= ROWS, ROWS * (2 - 2 * jnp.minimum(x, 3 - x)), 0)

    @pl.loop(0, GROUPS)
    def _(g):
        first, last = span_of(x, core, g)
        pos = first + offset
        d_first, d_last = jnp.int32(0), jnp.int32(0)
        for d in range(1, DOCS):
            d_first = d_first + (first >= bounds_ref[d]).astype(jnp.int32)
            d_last = d_last + (last >= bounds_ref[d]).astype(jnp.int32)
        starts_ref[g] = jnp.zeros((TALL, 128), jnp.int32)
        scales_ref[g] = jnp.zeros((TALL, 128), jnp.float32)

        def history(d, carry):
            begin = bounds_ref[d]
            end = jnp.where(d + 1 < DOCS, bounds_ref[jnp.minimum(d + 1, DOCS - 1)], PAIR * GROUPS)
            inside = pos >= begin
            size = jnp.full((TALL, 128), end - begin, jnp.int32).astype(jnp.float32)
            starts_ref[g] = jnp.where(inside, begin, starts_ref[g])
            scales_ref[g] = jnp.where(
                left, 0.0625, jnp.where(inside, lax.rsqrt(size), scales_ref[g])
            )
            return carry

        lax.fori_loop(d_first, d_last + 1, history, 0)


def buckets_kernel(where_ref, sums_ref, bias_ref, buckets):
    x, core = where_ref[0], where_ref[1]
    buckets[...] = jnp.zeros((NB, 8, 128), jnp.float32)

    @pl.loop(0, TALL // 16)
    def _(step):
        row = pl.multiple_of(step * 16, 16)
        near = [distance(x, core, c, row) for c in range(3)]
        totals = [jnp.zeros((8, 128), jnp.float32)] * NB
        for index, (c, e, low, high) in enumerate(SLABS):
            below, inside = edges_of(low, high)
            v = sums_ref[index + 1, pl.ds(row, 16), :]
            found = [(b, v[:8] + v[8:]) for edge, b in below]
            for edge, b in inside:
                part = jnp.where(near[c] >= edge - PAIR * e, v, 0.0)
                found.append((b, part[:8] + part[8:]))
            for k, (b, total) in enumerate(found):
                totals[b] = totals[b] + total
                if k:
                    totals[found[k - 1][0]] = totals[found[k - 1][0]] - total
        for b in range(NB):
            buckets[b] += totals[b]

    lane = lax.broadcasted_iota(jnp.int32, (8, 128), 1)
    row = jnp.zeros((8, 128), jnp.float32)
    for b in range(NB):
        total = jnp.sum(jnp.sum(buckets[b], axis=0, keepdims=True), axis=1, keepdims=True)
        row = jnp.where(lane == b, total * 0.5, row)
    bias_ref[...] = row


def main_kernel(
    where_ref, plan_ref, table, starts, scales, own_ref, kvx_ref, kvc_ref, kvxc_ref, qgx_ref,
    keep_ref, give_ref, mine_ref, theirs_ref, biasacc,
    line, dkv, acc, lhs, qgt, *stages,
):
    x = where_ref[0]
    core = where_ref[1]
    odd = lax.rem(x, 2)
    lower = jnp.minimum(x, 3 - x)

    def aligned(v):
        return pl.multiple_of(v * ROWS, ROWS)

    k_own = aligned(2 * core + odd)
    k_x = aligned(2 * core + 1 - odd)
    k_core = aligned(2 * (1 - core) + odd)
    k_both = aligned(2 * (1 - core) + 1 - odd)
    q_own = aligned((x != lower).astype(jnp.int32))
    q_x = aligned((x == lower).astype(jnp.int32))
    lane = lax.broadcasted_iota(jnp.int32, (TALL, 128), 1)
    left = lane < HD

    def chunk(k):
        return pl.ds(pl.multiple_of(CHUNK * k, CHUNK), CHUNK)

    def block(n, at):
        return pl.ds(pl.multiple_of(SUPER * n + at, ROWS), ROWS)

    @pl.loop(0, GROUPS, unroll=8)
    def _(n):
        line[block(n, k_own), :] = own_ref[n, :ROWS]
        line[block(n, k_x), :] = kvx_ref[n]
        line[block(n, k_core), :] = kvc_ref[n]
        line[block(n, k_both), :] = kvxc_ref[n]
        for c in range(3):
            dkv[3 * n + c] = jnp.zeros((128, CHUNK), jnp.float32)
        acc[n] = jnp.zeros((TALL, 128), jnp.float32)
        zero = jnp.zeros((ROWS, 128), jnp.bfloat16)
        for at, qg in ((q_own, own_ref[n, ROWS:]), (q_x, qgx_ref[n])):
            lhs[n, pl.ds(at, ROWS), :] = jnp.where(left[:ROWS], qg, zero)
            lhs[n, pl.ds(pl.multiple_of(at + TALL, ROWS), ROWS), :] = jnp.where(left[:ROWS], zero, qg)
        qgt[n] = (lhs[n, pl.ds(0, TALL), :] + lhs[n, pl.ds(TALL, TALL), :]).T

    @pl.loop(0, len(SLABS) + 1, unroll=7)
    def _(e):
        biasacc[e] = jnp.zeros((TALL, CHUNK), jnp.float32)

    score, weight = stages[:DEPTH], stages[DEPTH:]
    weight[0][...] = jnp.zeros((2 * TALL, WIDE), jnp.bfloat16)
    lanes = lax.broadcasted_iota(jnp.int32, (1, CHUNK), 1)
    places = [key_place(x, c, lanes) for c in range(3)]
    halves = (slice(0, CHUNK), slice(CHUNK, WIDE))

    def entry(k):
        chunks = [plan_ref[SLOTS + 2 * k + half] for half in range(2)]
        slabs = [plan_ref[3 * SLOTS + 2 * k + half] for half in range(2)]
        return plan_ref[k], chunks, slabs

    def scores(k, s):
        g, chunks, slabs = entry(k)
        keyvals = jnp.concatenate([line[chunk(n), :] for n in chunks], axis=0)
        for rows in (pl.ds(0, TALL), pl.ds(TALL, TALL)):
            s[rows, :] = lax.dot_general(
                lhs[g, rows, :], keyvals, NT, preferred_element_type=jnp.float32
            )

    def weigh(k, s, w_out):
        g, chunks, slabs = entry(k)
        for cols, n, e in zip(halves, chunks, slabs):
            pair = lax.div(n, 3)
            c = n - 3 * pair
            key = PAIR * pair + jnp.where(c == 0, places[0], jnp.where(c == 1, places[1], places[2]))
            half = s[pl.ds(0, TALL), cols] + table[e]
            half = jnp.where(key >= starts[g], half, LOW)
            t = jnp.tanh(half)
            u = 1.0 + t
            w = half * u
            ds = s[pl.ds(TALL, TALL), cols] * (u + w * (1.0 - t))
            biasacc[e] += ds
            w_out[pl.ds(0, TALL), cols] = w.astype(jnp.bfloat16)
            w_out[pl.ds(TALL, TALL), cols] = ds.astype(jnp.bfloat16)

    def gather(k, w_in):
        g, chunks, slabs = entry(k)
        keyvals = jnp.concatenate([line[chunk(n), :] for n in chunks], axis=0)
        od = jnp.dot(w_in[...], keyvals, preferred_element_type=jnp.float32)
        acc[g] += jnp.where(left, od[TALL:], od[:TALL])
        for rows, low in ((pl.ds(0, HD), TALL), (pl.ds(HD, HD), 0)):
            part = jnp.dot(
                qgt[g, rows, :], w_in[pl.ds(low, TALL), :], preferred_element_type=jnp.float32
            )
            for cols, n in zip(halves, chunks):
                dkv[n, rows, :] += part[:, cols]

    scores(1, score[1])

    @pl.loop(0, lax.div(plan_ref[5 * SLOTS] + DEPTH, DEPTH))
    def _(step):
        for i in range(DEPTH):
            k = DEPTH * step + i
            now, later = (i + 1) % DEPTH, (i + 2) % DEPTH
            gather(k, weight[i])
            weigh(k + 1, score[now], weight[now])
            scores(k + 2, score[later])

    @pl.loop(0, GROUPS, unroll=4)
    def _(n):
        for c in range(3):
            line[chunk(3 * n + c), :] = dkv[3 * n + c].astype(jnp.bfloat16).T
        acc[n] = acc[n] * scales[n]
        mine_ref[n] = acc[n, pl.ds(q_own, ROWS), :]
        theirs_ref[n] = acc[n, pl.ds(q_x, ROWS), :].astype(jnp.bfloat16)
        keep_ref[n, :ROWS] = line[block(n, k_own), :]
        keep_ref[n, ROWS:] = line[block(n, k_x), :]
        give_ref[n, :ROWS] = line[block(n, k_core), :]
        give_ref[n, ROWS:] = line[block(n, k_both), :]


def combine_kernel(mine_ref, got_qo_ref, dkv_ref, got_dkv_ref, out_ref):
    @pl.loop(0, GROUPS, unroll=4)
    def _(n):
        qo = mine_ref[n] + got_qo_ref[n].astype(jnp.float32)
        out_ref[n, :ROWS] = qo.astype(jnp.bfloat16)
        dkv = dkv_ref[n, :ROWS] + got_dkv_ref[n].astype(jnp.float32)
        out_ref[n, ROWS : 2 * ROWS] = dkv.astype(jnp.bfloat16)


def bias_kernel(in_ref, b0_ref, b1_ref, b2_ref, b3_ref, out_ref, terms_ref, sem):
    total = b0_ref[...] + b1_ref[...] + b2_ref[...] + b3_ref[...]
    high = total.astype(jnp.bfloat16)
    rest = total - high.astype(jnp.float32)
    middle = rest.astype(jnp.bfloat16)
    low = rest - middle.astype(jnp.float32)
    row = lax.broadcasted_iota(jnp.int32, (8, 128), 0)
    terms = jnp.where(
        row == 0,
        high.astype(jnp.float32),
        jnp.where(row == 1, middle.astype(jnp.float32), jnp.where(row == 2, low, 0.0)),
    )
    terms = jnp.concatenate([terms, jnp.zeros((8, 128), jnp.float32)], axis=0)
    for n in range(GROUPS):
        terms_ref[n] = terms.astype(jnp.bfloat16)
    copy = pltpu.make_async_copy(terms_ref, out_ref.at[:, pl.ds(2 * ROWS, 16), :], sem)
    copy.start()
    copy.wait()


def unpack_kernel(in_ref, out_ref, grad_ref):
    for h in range(0, H, 2):
        cols = slice(h * HD, (h + 2) * HD)
        a, b = in_ref[h, :ROWS], in_ref[h + 1, :ROWS]
        grad_ref[0, :, cols] = jnp.concatenate([a[:, :HD], b[:, :HD]], axis=1)
        out_ref[:, cols] = jnp.concatenate([a[:, HD:], b[:, HD:]], axis=1)
        a, b = in_ref[h, ROWS : 2 * ROWS], in_ref[h + 1, ROWS : 2 * ROWS]
        grad_ref[1, :, cols] = jnp.concatenate([a[:, :HD], b[:, :HD]], axis=1)
        grad_ref[2, :, cols] = jnp.concatenate([a[:, HD:], b[:, HD:]], axis=1)


def swap(v, axis, partner):
    return lax.ppermute(v, axis, [(i, p) for i, p in enumerate(partner)])


def per_device(qkv, grad_out, rab, doc_ids):
    bf16, f32 = jnp.bfloat16, jnp.float32
    x, y, z, core = (lax.axis_index(a) for a in ("x", "y", "z", "core"))
    whole = pl.BlockSpec(memory_space=VMEM)
    scalars = pl.BlockSpec(memory_space=SMEM)
    block = jax.ShapeDtypeStruct((H, ROWS, 128), bf16)
    double = jax.ShapeDtypeStruct((H, 2 * ROWS, 128), bf16)
    slabs = jax.ShapeDtypeStruct((len(SLABS) + 1, TALL, CHUNK), f32)
    small = pltpu.CompilerParams(vmem_limit_bytes=8 * 2**20)
    large = pltpu.CompilerParams(vmem_limit_bytes=34 * 2**20)
    first_row = (((y * 4 + z) * 2 + core) * 4 + x) * ROWS
    where = jnp.stack([x, core])
    packed, bounds = pl.pallas_call(
        pack_kernel,
        out_shape=(double, jax.ShapeDtypeStruct((DOCS,), jnp.int32)),
        in_specs=[scalars] + [pl.BlockSpec(memory_space=pltpu.HBM)] * 3,
        out_specs=(whole, scalars),
        scratch_shapes=[
            VMEM((96, 128), jnp.int32),
            VMEM((3, ROWS, H * HD), bf16),
            VMEM((ROWS, H * HD), bf16),
            pltpu.SemaphoreType.DMA((3,)),
        ],
        compiler_params=pltpu.CompilerParams(vmem_limit_bytes=63 * 2**20),
        name="pack",
    )(first_row.reshape(1), doc_ids.reshape(96, 128), qkv.transpose(1, 0, 2), grad_out)
    own = lax.all_to_all(packed, ("y", "z"), 0, 0, tiled=True)
    kv_own, qg_own = own[:, :ROWS], own[:, ROWS:]
    qg_x = swap(qg_own, "x", (3, 2, 1, 0))
    kv_x = swap(kv_own, "x", (1, 0, 3, 2))
    kv_core = swap(kv_own, "core", (1, 0))
    table_row = lax.dynamic_slice_in_dim(rab, y * 4 + z, 1, 0)[0]
    table, starts, scales, plan = pl.pallas_call(
        table_kernel,
        out_shape=(
            slabs,
            jax.ShapeDtypeStruct((GROUPS, TALL, 128), jnp.int32),
            jax.ShapeDtypeStruct((GROUPS, TALL, 128), f32),
            jax.ShapeDtypeStruct((5 * SLOTS + 1,), jnp.int32),
        ),
        in_specs=[scalars] * 3,
        out_specs=(whole, whole, whole, scalars),
        compiler_params=small,
        cost_estimate=pl.CostEstimate(flops=0, bytes_accessed=0, transcendentals=0),
        name="table",
    )(where, table_row, bounds)
    kv_x, qg_x, table, starts, scales, plan = lax.optimization_barrier(
        (kv_x, qg_x, table, starts, scales, plan)
    )
    kv_both = swap(kv_x, "core", (1, 0))
    keep, give, mine, theirs, sums = pl.pallas_call(
        main_kernel,
        out_shape=[double, double, jax.ShapeDtypeStruct((H, ROWS, 128), f32), block, slabs],
        in_specs=[scalars] * 2 + [whole] * 8,
        out_specs=[whole] * 5,
        scratch_shapes=[
            VMEM((GROUPS * SUPER, 128), bf16),
            VMEM((3 * GROUPS, 128, CHUNK), f32),
            VMEM((GROUPS, TALL, 128), f32),
            VMEM((GROUPS, 2 * TALL, 128), bf16),
            VMEM((GROUPS, 128, TALL), bf16),
        ]
        + [VMEM((2 * TALL, WIDE), f32)] * DEPTH
        + [VMEM((2 * TALL, WIDE), bf16)] * DEPTH,
        compiler_params=large,
        name="attend",
    )(where, plan, table, starts, scales, own, kv_x, kv_core, kv_both, qg_x)
    got = swap(give, "core", (1, 0))
    dkv = keep.astype(f32) + got.astype(f32)
    dkv_x = dkv[:, ROWS:].astype(bf16)
    got_qo = swap(theirs, "x", (3, 2, 1, 0))
    got_dkv = swap(dkv_x, "x", (1, 0, 3, 2))
    bias = pl.pallas_call(
        buckets_kernel,
        out_shape=jax.ShapeDtypeStruct((8, 128), f32),
        in_specs=[scalars, whole],
        out_specs=whole,
        scratch_shapes=[VMEM((NB, 8, 128), f32)],
        compiler_params=small,
        cost_estimate=pl.CostEstimate(flops=0, bytes_accessed=0, transcendentals=0),
        name="buckets",
    )(where, sums)
    others = [swap(bias, "x", p) for p in ((1, 0, 3, 2), (3, 2, 1, 0), (2, 3, 0, 1))]
    results = pl.pallas_call(
        combine_kernel,
        out_shape=jax.ShapeDtypeStruct((H, 2 * ROWS + 16, 128), bf16),
        in_specs=[whole] * 4,
        out_specs=whole,
        compiler_params=small,
        cost_estimate=pl.CostEstimate(flops=0, bytes_accessed=10**7, transcendentals=0),
        name="combine",
    )(mine, got_qo, dkv, got_dkv)
    results = pl.pallas_call(
        bias_kernel,
        out_shape=jax.ShapeDtypeStruct((H, 2 * ROWS + 16, 128), bf16),
        in_specs=[pl.BlockSpec(memory_space=pl.ANY)] + [whole] * 4,
        out_specs=pl.BlockSpec(memory_space=pl.ANY),
        scratch_shapes=[VMEM((GROUPS, 16, 128), bf16), pltpu.SemaphoreType.DMA(())],
        input_output_aliases={0: 0},
        compiler_params=small,
        name="bias",
    )(results, bias, *others)
    results = lax.all_to_all(results, ("y", "z"), 0, 0, tiled=True)
    terms = lax.dynamic_slice(results, (x * 4, 2 * ROWS, 0), (4, 3, NB)).astype(f32)
    bias_grad = terms[:, 0] + terms[:, 1] + terms[:, 2]
    bias_grad = bias_grad + swap(bias_grad, "core", (1, 0))
    out, grad_qkv = pl.pallas_call(
        unpack_kernel,
        out_shape=(
            jax.ShapeDtypeStruct((ROWS, H * HD), bf16),
            jax.ShapeDtypeStruct((3, ROWS, H * HD), bf16),
        ),
        in_specs=[whole],
        out_specs=(whole, whole),
        compiler_params=small,
        name="unpack",
    )(results)
    return out, grad_qkv.transpose(1, 0, 2), bias_grad


def solution(mesh):
    fine = Mesh(mesh.devices.reshape(4, 4, 4, 2), ("x", "y", "z", "core"))
    rows = ("y", "z", "core", "x")
    return jax.shard_map(
        per_device,
        mesh=fine,
        in_specs=(P(rows, None, None), P(rows, None), P(), P()),
        out_specs=(P(rows, None), P(rows, None, None), P("x", None)),
        check_vma=False,
    )
```

```python
import jax
import jax.numpy as jnp
from jax import lax
from jax.experimental import pallas as pl
from jax.experimental.pallas import tpu as pltpu
from jax.sharding import Mesh
from jax.sharding import PartitionSpec as P

HD = 64
H = 16
NB = 20
DOCS = 8
ROWS = 96
SUPER = 384
GROUPS = 16
PAIR = 768
TALL = 192
WIDE = 256
CHUNK = 128
SLOTS = 256
DEPTH = 6
LOW = -1e30
VMEM = pltpu.VMEM
SMEM = pltpu.SMEM
NT = (((1,), (1,)), ((), ()))


def doc_bounds(ids):
    return [jnp.int32(0)] + [
        jnp.sum((ids < d).astype(jnp.float32)).astype(jnp.int32) for d in range(1, DOCS)
    ]


def pack_kernel(where_ref, ids, qkv, g_in, out_ref, bounds_ref, ids_ref, qkv_ref, g_ref, sems):
    copies = [
        pltpu.make_async_copy(source, target, sems.at[k])
        for k, (source, target) in enumerate(((ids, ids_ref), (qkv, qkv_ref), (g_in, g_ref)))
    ]
    for copy in copies:
        copy.start()
    copies[0].wait()
    bounds = doc_bounds(ids_ref[...])
    for d in range(DOCS):
        bounds_ref[d] = bounds[d]
    pos = where_ref[0] + lax.broadcasted_iota(jnp.int32, (ROWS, 128), 0)
    length = jnp.zeros((ROWS, 128), jnp.int32)
    ends = bounds[1:] + [jnp.int32(PAIR * GROUPS)]
    for d in range(DOCS):
        length = jnp.where(pos >= bounds[d], ends[d] - bounds[d], length)
    scale = lax.rsqrt(length.astype(jnp.float32))[:, :HD]
    copies[1].wait()
    copies[2].wait()
    for h in range(H):
        cols = slice(h * HD, (h + 1) * HD)
        out_ref[h, :ROWS] = jnp.concatenate([qkv_ref[1, :, cols], qkv_ref[2, :, cols]], axis=1)
        q = (qkv_ref[0, :, cols].astype(jnp.float32) * 0.0625).astype(jnp.bfloat16)
        g = (g_ref[:, cols].astype(jnp.float32) * scale).astype(jnp.bfloat16)
        out_ref[h, ROWS:] = jnp.concatenate([q, g], axis=1)


EDGES = [(k, k) for k in range(8)] + [(2**p, p + 6) for p in range(3, 13)]


def edges_of(low, high):
    below = [edge for edge in EDGES if edge[0] <= low]
    return below[-1:], [edge for edge in EDGES if low < edge[0] <= high]


def key_place(x, c, lane):
    j = CHUNK * c + lane
    return j + 2 * ROWS * lax.div(x, 2) + jnp.where(j >= 2 * ROWS, SUPER - 2 * ROWS, 0)


SLABS = [
    (c, e, PAIR * e - (319, 639, 767)[c], PAIR * e + PAIR - 1 - (0, 128, 448)[c])
    for c in range(3)
    for e in range(9)
]


def distance(x, core, c, row):
    i = row + lax.broadcasted_iota(jnp.int32, (16, CHUNK), 0)
    lane = lax.broadcasted_iota(jnp.int32, (16, CHUNK), 1)
    lower = jnp.minimum(x, 3 - x)
    i = i + ROWS * lower + jnp.where(i >= ROWS, ROWS * (2 - 2 * lower), 0)
    return SUPER * core + i - key_place(x, c, lane)


def start_of(bounds_ref, pos):
    start = jnp.int32(0)
    for d in range(1, DOCS):
        start = jnp.where(pos >= bounds_ref[d], bounds_ref[d], start)
    return start


def span_of(x, core, g):
    lower = jnp.minimum(x, 3 - x)
    base = PAIR * g + SUPER * core
    return base + ROWS * lower, base + ROWS * (4 - lower) - 1


def table_kernel(where_ref, rab_ref, bounds_ref, table_ref, starts_ref, scales_ref, plan_ref):
    x, core = where_ref[0], where_ref[1]
    column = 2 * ROWS * lax.div(x, 2)

    def of_group(g, at):
        first, last = span_of(x, core, g)
        begin = start_of(bounds_ref, first)

        def of_pair(n, at):
            for c, (low, high) in enumerate(((0, 127), (128, 447), (448, 575))):
                place = PAIR * n + column
                live = (place + high >= begin) & (place + low <= last)
                plan_ref[lax.div(at, 2)] = g
                plan_ref[SLOTS + at] = 3 * n + c
                plan_ref[3 * SLOTS + at] = 9 * c + g - n + 1
                at = at + live.astype(jnp.int32)
            return at

        at = lax.fori_loop(lax.div(begin, PAIR), g + 1, of_pair, at)
        plan_ref[SLOTS + at] = 0
        plan_ref[3 * SLOTS + at] = 0
        return at + lax.rem(at, 2)

    at = lax.fori_loop(0, GROUPS, of_group, jnp.int32(2))
    tiles = lax.div(at, 2)
    plan_ref[5 * SLOTS] = tiles - 1
    plan_ref[0] = 0
    for extra in range(DEPTH + 1):
        plan_ref[tiles + extra] = 0
    for half in range(2):
        plan_ref[SLOTS + half] = 0
        plan_ref[3 * SLOTS + half] = 0
        for extra in range(DEPTH + 1):
            plan_ref[SLOTS + at + 2 * extra + half] = 0
            plan_ref[3 * SLOTS + at + 2 * extra + half] = 0

    table_ref[0] = jnp.full((TALL, CHUNK), LOW, jnp.float32)

    @pl.loop(0, TALL // 16)
    def _(step):
        row = pl.multiple_of(step * 16, 16)
        near = [distance(x, core, c, row) for c in range(3)]
        for index, (c, e, low, high) in enumerate(SLABS):
            below, inside = edges_of(low, high)
            value = jnp.full((16, CHUNK), rab_ref[below[0][1]] * 0.5 if below else LOW, jnp.float32)
            for edge, b in inside:
                value = jnp.where(near[c] >= edge - PAIR * e, rab_ref[b] * 0.5, value)
            table_ref[index + 1, pl.ds(row, 16), :] = value

    left = lax.broadcasted_iota(jnp.int32, (TALL, 128), 1) < HD
    row = lax.broadcasted_iota(jnp.int32, (TALL, 128), 0)
    offset = row + jnp.where(row >= ROWS, ROWS * (2 - 2 * jnp.minimum(x, 3 - x)), 0)

    @pl.loop(0, GROUPS)
    def _(g):
        first, last = span_of(x, core, g)
        pos = first + offset
        d_first, d_last = jnp.int32(0), jnp.int32(0)
        for d in range(1, DOCS):
            d_first = d_first + (first >= bounds_ref[d]).astype(jnp.int32)
            d_last = d_last + (last >= bounds_ref[d]).astype(jnp.int32)
        starts_ref[g] = jnp.zeros((TALL, 128), jnp.int32)
        scales_ref[g] = jnp.zeros((TALL, 128), jnp.float32)

        def history(d, carry):
            begin = bounds_ref[d]
            end = jnp.where(d + 1 < DOCS, bounds_ref[jnp.minimum(d + 1, DOCS - 1)], PAIR * GROUPS)
            inside = pos >= begin
            size = jnp.full((TALL, 128), end - begin, jnp.int32).astype(jnp.float32)
            starts_ref[g] = jnp.where(inside, begin, starts_ref[g])
            scales_ref[g] = jnp.where(
                left, 0.0625, jnp.where(inside, lax.rsqrt(size), scales_ref[g])
            )
            return carry

        lax.fori_loop(d_first, d_last + 1, history, 0)


def buckets_kernel(where_ref, sums_ref, bias_ref, buckets):
    x, core = where_ref[0], where_ref[1]
    buckets[...] = jnp.zeros((NB, 8, 128), jnp.float32)

    @pl.loop(0, TALL // 16)
    def _(step):
        row = pl.multiple_of(step * 16, 16)
        near = [distance(x, core, c, row) for c in range(3)]
        totals = [jnp.zeros((8, 128), jnp.float32)] * NB
        for index, (c, e, low, high) in enumerate(SLABS):
            below, inside = edges_of(low, high)
            v = sums_ref[index + 1, pl.ds(row, 16), :]
            found = [(b, v[:8] + v[8:]) for edge, b in below]
            for edge, b in inside:
                part = jnp.where(near[c] >= edge - PAIR * e, v, 0.0)
                found.append((b, part[:8] + part[8:]))
            for k, (b, total) in enumerate(found):
                totals[b] = totals[b] + total
                if k:
                    totals[found[k - 1][0]] = totals[found[k - 1][0]] - total
        for b in range(NB):
            buckets[b] += totals[b]

    lane = lax.broadcasted_iota(jnp.int32, (8, 128), 1)
    row = jnp.zeros((8, 128), jnp.float32)
    for b in range(NB):
        total = jnp.sum(jnp.sum(buckets[b], axis=0, keepdims=True), axis=1, keepdims=True)
        row = jnp.where(lane == b, total * 0.5, row)
    bias_ref[...] = row


def main_kernel(
    where_ref, plan_ref, table, starts, scales, own_ref, kvx_ref, kvc_ref, kvxc_ref, qgx_ref,
    keep_ref, give_ref, mine_ref, theirs_ref, biasacc,
    line, dkv, acc, lhs, qgt, *stages,
):
    x = where_ref[0]
    core = where_ref[1]
    odd = lax.rem(x, 2)
    lower = jnp.minimum(x, 3 - x)

    def aligned(v):
        return pl.multiple_of(v * ROWS, ROWS)

    k_own = aligned(2 * core + odd)
    k_x = aligned(2 * core + 1 - odd)
    k_core = aligned(2 * (1 - core) + odd)
    k_both = aligned(2 * (1 - core) + 1 - odd)
    q_own = aligned((x != lower).astype(jnp.int32))
    q_x = aligned((x == lower).astype(jnp.int32))
    lane = lax.broadcasted_iota(jnp.int32, (TALL, 128), 1)
    left = lane < HD

    def chunk(k):
        return pl.ds(pl.multiple_of(CHUNK * k, CHUNK), CHUNK)

    def block(n, at):
        return pl.ds(pl.multiple_of(SUPER * n + at, ROWS), ROWS)

    @pl.loop(0, GROUPS, unroll=8)
    def _(n):
        line[block(n, k_own), :] = own_ref[n, :ROWS]
        line[block(n, k_x), :] = kvx_ref[n]
        line[block(n, k_core), :] = kvc_ref[n]
        line[block(n, k_both), :] = kvxc_ref[n]
        for c in range(3):
            dkv[3 * n + c] = jnp.zeros((128, CHUNK), jnp.float32)
        acc[n] = jnp.zeros((TALL, 128), jnp.float32)
        zero = jnp.zeros((ROWS, 128), jnp.bfloat16)
        for at, qg in ((q_own, own_ref[n, ROWS:]), (q_x, qgx_ref[n])):
            lhs[n, pl.ds(at, ROWS), :] = jnp.where(left[:ROWS], qg, zero)
            lhs[n, pl.ds(pl.multiple_of(at + TALL, ROWS), ROWS), :] = jnp.where(left[:ROWS], zero, qg)
        qgt[n] = (lhs[n, pl.ds(0, TALL), :] + lhs[n, pl.ds(TALL, TALL), :]).T

    @pl.loop(0, len(SLABS) + 1, unroll=7)
    def _(e):
        biasacc[e] = jnp.zeros((TALL, CHUNK), jnp.float32)

    score, weight = stages[:DEPTH], stages[DEPTH:]
    weight[0][...] = jnp.zeros((2 * TALL, WIDE), jnp.bfloat16)
    lanes = lax.broadcasted_iota(jnp.int32, (1, CHUNK), 1)
    places = [key_place(x, c, lanes) for c in range(3)]
    halves = (slice(0, CHUNK), slice(CHUNK, WIDE))

    def entry(k):
        chunks = [plan_ref[SLOTS + 2 * k + half] for half in range(2)]
        slabs = [plan_ref[3 * SLOTS + 2 * k + half] for half in range(2)]
        return plan_ref[k], chunks, slabs

    def scores(k, s):
        g, chunks, slabs = entry(k)
        keyvals = jnp.concatenate([line[chunk(n), :] for n in chunks], axis=0)
        for rows in (pl.ds(0, TALL), pl.ds(TALL, TALL)):
            s[rows, :] = lax.dot_general(
                lhs[g, rows, :], keyvals, NT, preferred_element_type=jnp.float32
            )

    def weigh(k, s, w_out):
        g, chunks, slabs = entry(k)
        for cols, n, e in zip(halves, chunks, slabs):
            pair = lax.div(n, 3)
            c = n - 3 * pair
            key = PAIR * pair + jnp.where(c == 0, places[0], jnp.where(c == 1, places[1], places[2]))
            half = s[pl.ds(0, TALL), cols] + table[e]
            half = jnp.where(key >= starts[g], half, LOW)
            t = jnp.tanh(half)
            u = 1.0 + t
            w = half * u
            ds = s[pl.ds(TALL, TALL), cols] * (u + w * (1.0 - t))
            biasacc[e] += ds
            w_out[pl.ds(0, TALL), cols] = w.astype(jnp.bfloat16)
            w_out[pl.ds(TALL, TALL), cols] = ds.astype(jnp.bfloat16)

    def gather(k, w_in):
        g, chunks, slabs = entry(k)
        keyvals = jnp.concatenate([line[chunk(n), :] for n in chunks], axis=0)
        od = jnp.dot(w_in[...], keyvals, preferred_element_type=jnp.float32)
        acc[g] += jnp.where(left, od[TALL:], od[:TALL])
        for rows, low in ((pl.ds(0, HD), TALL), (pl.ds(HD, HD), 0)):
            part = jnp.dot(
                qgt[g, rows, :], w_in[pl.ds(low, TALL), :], preferred_element_type=jnp.float32
            )
            for cols, n in zip(halves, chunks):
                dkv[n, rows, :] += part[:, cols]

    scores(1, score[1])

    @pl.loop(0, lax.div(plan_ref[5 * SLOTS] + DEPTH, DEPTH))
    def _(step):
        for i in range(DEPTH):
            k = DEPTH * step + i
            now, later = (i + 1) % DEPTH, (i + 2) % DEPTH
            gather(k, weight[i])
            weigh(k + 1, score[now], weight[now])
            scores(k + 2, score[later])

    @pl.loop(0, GROUPS, unroll=4)
    def _(n):
        for c in range(3):
            line[chunk(3 * n + c), :] = dkv[3 * n + c].astype(jnp.bfloat16).T
        acc[n] = acc[n] * scales[n]
        mine_ref[n] = acc[n, pl.ds(q_own, ROWS), :]
        theirs_ref[n] = acc[n, pl.ds(q_x, ROWS), :].astype(jnp.bfloat16)
        keep_ref[n, :ROWS] = line[block(n, k_own), :]
        keep_ref[n, ROWS:] = line[block(n, k_x), :]
        give_ref[n, :ROWS] = line[block(n, k_core), :]
        give_ref[n, ROWS:] = line[block(n, k_both), :]


def combine_kernel(mine_ref, got_qo_ref, keep_ref, got_ref, got_dkv_ref, out_ref):
    @pl.loop(0, GROUPS, unroll=4)
    def _(n):
        qo = mine_ref[n] + got_qo_ref[n].astype(jnp.float32)
        out_ref[n, :ROWS] = qo.astype(jnp.bfloat16)
        dkv = keep_ref[n, :ROWS].astype(jnp.float32) + got_ref[n, :ROWS].astype(jnp.float32)
        dkv = dkv + got_dkv_ref[n].astype(jnp.float32)
        out_ref[n, ROWS : 2 * ROWS] = dkv.astype(jnp.bfloat16)


def bias_kernel(in_ref, b0_ref, b1_ref, b2_ref, b3_ref, out_ref, terms_ref, sem):
    total = b0_ref[...] + b1_ref[...] + b2_ref[...] + b3_ref[...]
    high = total.astype(jnp.bfloat16)
    rest = total - high.astype(jnp.float32)
    middle = rest.astype(jnp.bfloat16)
    low = rest - middle.astype(jnp.float32)
    row = lax.broadcasted_iota(jnp.int32, (8, 128), 0)
    terms = jnp.where(
        row == 0,
        high.astype(jnp.float32),
        jnp.where(row == 1, middle.astype(jnp.float32), jnp.where(row == 2, low, 0.0)),
    )
    terms = jnp.concatenate([terms, jnp.zeros((8, 128), jnp.float32)], axis=0)
    for n in range(GROUPS):
        terms_ref[n] = terms.astype(jnp.bfloat16)
    copy = pltpu.make_async_copy(terms_ref, out_ref.at[:, pl.ds(2 * ROWS, 16), :], sem)
    copy.start()
    copy.wait()


def unpack_kernel(in_ref, out_ref, grad_ref):
    for h in range(0, H, 2):
        cols = slice(h * HD, (h + 2) * HD)
        a, b = in_ref[h, :ROWS], in_ref[h + 1, :ROWS]
        grad_ref[0, :, cols] = jnp.concatenate([a[:, :HD], b[:, :HD]], axis=1)
        out_ref[:, cols] = jnp.concatenate([a[:, HD:], b[:, HD:]], axis=1)
        a, b = in_ref[h, ROWS : 2 * ROWS], in_ref[h + 1, ROWS : 2 * ROWS]
        grad_ref[1, :, cols] = jnp.concatenate([a[:, :HD], b[:, :HD]], axis=1)
        grad_ref[2, :, cols] = jnp.concatenate([a[:, HD:], b[:, HD:]], axis=1)


def swap(v, axis, partner):
    return lax.ppermute(v, axis, [(i, p) for i, p in enumerate(partner)])


def per_device(qkv, grad_out, rab, doc_ids):
    bf16, f32 = jnp.bfloat16, jnp.float32
    x, y, z, core = (lax.axis_index(a) for a in ("x", "y", "z", "core"))
    whole = pl.BlockSpec(memory_space=VMEM)
    scalars = pl.BlockSpec(memory_space=SMEM)
    block = jax.ShapeDtypeStruct((H, ROWS, 128), bf16)
    double = jax.ShapeDtypeStruct((H, 2 * ROWS, 128), bf16)
    slabs = jax.ShapeDtypeStruct((len(SLABS) + 1, TALL, CHUNK), f32)
    small = pltpu.CompilerParams(vmem_limit_bytes=8 * 2**20)
    large = pltpu.CompilerParams(vmem_limit_bytes=34 * 2**20)
    first_row = (((y * 4 + z) * 2 + core) * 4 + x) * ROWS
    where = jnp.stack([x, core])
    packed, bounds = pl.pallas_call(
        pack_kernel,
        out_shape=(double, jax.ShapeDtypeStruct((DOCS,), jnp.int32)),
        in_specs=[scalars] + [pl.BlockSpec(memory_space=pltpu.HBM)] * 3,
        out_specs=(whole, scalars),
        scratch_shapes=[
            VMEM((96, 128), jnp.int32),
            VMEM((3, ROWS, H * HD), bf16),
            VMEM((ROWS, H * HD), bf16),
            pltpu.SemaphoreType.DMA((3,)),
        ],
        compiler_params=pltpu.CompilerParams(vmem_limit_bytes=63 * 2**20),
        name="pack",
    )(first_row.reshape(1), doc_ids.reshape(96, 128), qkv.transpose(1, 0, 2), grad_out)
    own = lax.all_to_all(packed, ("y", "z"), 0, 0, tiled=True)
    kv_own, qg_own = own[:, :ROWS], own[:, ROWS:]
    qg_x = swap(qg_own, "x", (3, 2, 1, 0))
    kv_x = swap(kv_own, "x", (1, 0, 3, 2))
    kv_core = swap(kv_own, "core", (1, 0))
    table_row = lax.dynamic_slice_in_dim(rab, y * 4 + z, 1, 0)[0]
    table, starts, scales, plan = pl.pallas_call(
        table_kernel,
        out_shape=(
            slabs,
            jax.ShapeDtypeStruct((GROUPS, TALL, 128), jnp.int32),
            jax.ShapeDtypeStruct((GROUPS, TALL, 128), f32),
            jax.ShapeDtypeStruct((5 * SLOTS + 1,), jnp.int32),
        ),
        in_specs=[scalars] * 3,
        out_specs=(whole, whole, whole, scalars),
        compiler_params=small,
        cost_estimate=pl.CostEstimate(flops=0, bytes_accessed=0, transcendentals=0),
        name="table",
    )(where, table_row, bounds)
    kv_x, qg_x, table, starts, scales, plan = lax.optimization_barrier(
        (kv_x, qg_x, table, starts, scales, plan)
    )
    kv_both = swap(kv_x, "core", (1, 0))
    keep, give, mine, theirs, sums = pl.pallas_call(
        main_kernel,
        out_shape=[double, double, jax.ShapeDtypeStruct((H, ROWS, 128), f32), block, slabs],
        in_specs=[scalars] * 2 + [whole] * 8,
        out_specs=[whole] * 5,
        scratch_shapes=[
            VMEM((GROUPS * SUPER, 128), bf16),
            VMEM((3 * GROUPS, 128, CHUNK), f32),
            VMEM((GROUPS, TALL, 128), f32),
            VMEM((GROUPS, 2 * TALL, 128), bf16),
            VMEM((GROUPS, 128, TALL), bf16),
        ]
        + [VMEM((2 * TALL, WIDE), f32)] * DEPTH
        + [VMEM((2 * TALL, WIDE), bf16)] * DEPTH,
        compiler_params=large,
        name="attend",
    )(where, plan, table, starts, scales, own, kv_x, kv_core, kv_both, qg_x)
    got = swap(give, "core", (1, 0))
    dkv_x = (keep[:, ROWS:].astype(f32) + got[:, ROWS:].astype(f32)).astype(bf16)
    got_qo = swap(theirs, "x", (3, 2, 1, 0))
    got_dkv = swap(dkv_x, "x", (1, 0, 3, 2))
    bias = pl.pallas_call(
        buckets_kernel,
        out_shape=jax.ShapeDtypeStruct((8, 128), f32),
        in_specs=[scalars, whole],
        out_specs=whole,
        scratch_shapes=[VMEM((NB, 8, 128), f32)],
        compiler_params=small,
        cost_estimate=pl.CostEstimate(flops=0, bytes_accessed=0, transcendentals=0),
        name="buckets",
    )(where, sums)
    others = [swap(bias, "x", p) for p in ((1, 0, 3, 2), (3, 2, 1, 0), (2, 3, 0, 1))]
    results = pl.pallas_call(
        combine_kernel,
        out_shape=jax.ShapeDtypeStruct((H, 2 * ROWS + 16, 128), bf16),
        in_specs=[whole] * 5,
        out_specs=whole,
        compiler_params=small,
        cost_estimate=pl.CostEstimate(flops=0, bytes_accessed=10**7, transcendentals=0),
        name="combine",
    )(mine, got_qo, keep, got, got_dkv)
    results = pl.pallas_call(
        bias_kernel,
        out_shape=jax.ShapeDtypeStruct((H, 2 * ROWS + 16, 128), bf16),
        in_specs=[pl.BlockSpec(memory_space=pl.ANY)] + [whole] * 4,
        out_specs=pl.BlockSpec(memory_space=pl.ANY),
        scratch_shapes=[VMEM((GROUPS, 16, 128), bf16), pltpu.SemaphoreType.DMA(())],
        input_output_aliases={0: 0},
        compiler_params=small,
        name="bias",
    )(results, bias, *others)
    results = lax.all_to_all(results, ("y", "z"), 0, 0, tiled=True)
    terms = lax.dynamic_slice(results, (x * 4, 2 * ROWS, 0), (4, 3, NB)).astype(f32)
    bias_grad = terms[:, 0] + terms[:, 1] + terms[:, 2]
    bias_grad = bias_grad + swap(bias_grad, "core", (1, 0))
    out, grad_qkv = pl.pallas_call(
        unpack_kernel,
        out_shape=(
            jax.ShapeDtypeStruct((ROWS, H * HD), bf16),
            jax.ShapeDtypeStruct((3, ROWS, H * HD), bf16),
        ),
        in_specs=[whole],
        out_specs=(whole, whole),
        compiler_params=small,
        name="unpack",
    )(results)
    return out, grad_qkv.transpose(1, 0, 2), bias_grad


def solution(mesh):
    fine = Mesh(mesh.devices.reshape(4, 4, 4, 2), ("x", "y", "z", "core"))
    rows = ("y", "z", "core", "x")
    return jax.shard_map(
        per_device,
        mesh=fine,
        in_specs=(P(rows, None, None), P(rows, None), P(), P()),
        out_specs=(P(rows, None), P(rows, None, None), P("x", None)),
        check_vma=False,
    )
```
